256 devices in a mesh: rep: 16 (over z_lo, y), exp: 16 (over z_hi, x, core).
Axes of the slice: x: 4, y: 4, z: 8 (z_hi: 2, z_lo: 4; z = z_hi * 4 + z_lo), core: 2. Of those that a mesh axis runs over, the one named last changes fastest.
Arguments:
- tokens: bfloat16 [16, 2048, 2048], P('rep', 'exp'), may hold values from -6 to 6
- cotangent: bfloat16 [16, 2048, 2048], P('rep', 'exp'), may hold values from -6 to 6
- routes: int32 [16, 2048, 8], P('rep', 'exp'), may hold values from 0 to 15, all different within a row; in each aligned block of 128 rows (0 to 127, 128 to 255, ..., all dimensions but the last counted through in order) at most 72 rows name the same one
- route_weights: float32 [16, 2048, 8], P('rep', 'exp'), may hold values from 0.05 to 0.5
- gate_weight: bfloat16 [16, 16, 2048, 512], P('rep', 'exp'), may hold values from -6 to 6
- up_weight: bfloat16 [16, 16, 2048, 512], P('rep', 'exp'), may hold values from -6 to 6
- down_weight: bfloat16 [16, 16, 512, 2048], P('rep', 'exp'), may hold values from -6 to 6
Outputs:
- mixed_gate: bfloat16 [16, 16, 1024, 512], P('rep', 'exp')
- mixed_up: bfloat16 [16, 16, 1024, 512], P('rep', 'exp')
- mixed_down: bfloat16 [16, 16, 256, 2048], P('rep', 'exp')
The draws below stay inside these ranges and needn't reach their ends.
Inputs may be any that keep to these rules, and one draw needn't show every extreme that they name: Within the 128 tokens of one device no expert is named by more than 72 routes, and some device's tokens reach 72 for some expert; a token's 8 ids are distinct.
All inputs are finite; a program needn't handle non-finite values.
Results may differ from the reference program's by a relative error of at most 0.0058.
Values may be sent and summed in bfloat16 or wider, within the bound.
No kernel may reach another device: no remote copies, remote signals or barrier semaphores. Data moves between devices by JAX's collectives and lax.ppermute only.
A program may use at most 128 MiB of HBM per device.

```python
import math
import jax
import jax.numpy as jnp
import numpy as np
from jax import lax

D = 2048
FF = 512
TOK_DEV = 128
ROUND = 2
EXPERTS = 16
TOP = 8
CAP = 72
TOKENS = 2048
REPS = 16
N_EXP = 16


def block_scale(rng, dims, pieces, smallest, largest):
    gain = 1.0
    for dim, shards_of in pieces:
        heights = jax.random.uniform(jax.random.fold_in(jax.random.fold_in(rng, 6), dim), (shards_of,), jnp.float32, smallest / len(pieces), largest / len(pieces))
        gain = gain * jnp.repeat(jnp.exp(heights), dims[dim] // shards_of).reshape((-1,) + (1,) * (len(dims) - 1 - dim))
    return gain


def routed_block(own_key, own, number, rows, number_of, top, limit, lean):
    sequence = jax.random.permutation(own_key, number_of)
    packed, ordinary = portions_of(number_of, rows * top, limit, lean, True), portions_of(number_of, rows * top, limit, lean, False)
    places = jnp.arange(number_of)

    def named(tallies, offset_by):
        used = int((tallies > 0).sum())
        fixed = max(1, used // 4)
        shifted = fixed + (places - fixed + offset_by * (used - fixed)) % max(1, number_of - fixed)
        return jnp.zeros((number_of,), jnp.int32).at[sequence[jnp.where(places < fixed, places, shifted)]].set(jnp.asarray(tallies, jnp.int32))

    tallies = jnp.where(number % 4 == 0, named(packed, number // 4), named(ordinary, number - number // 4 - 1))
    mixed = jax.random.permutation(jax.random.fold_in(own, 3), number_of)
    source_of, sink = mixed[0:number_of // 2 * 2:2], mixed[1:number_of // 2 * 2:2]
    margin = jnp.minimum(tallies[source_of] - 1, limit - tallies[sink]) // 2
    margin = jnp.where((source_of == sequence[0]) | (sink == sequence[0]) | (tallies[sink] == 0), 0, jnp.maximum(margin, 0))
    shifted = jax.random.randint(jax.random.fold_in(own, 4), (number_of // 2,), 0, 1 << 20) % (margin + 1)
    tallies = tallies.at[source_of].add(-shifted).at[sink].add(shifted)
    labels = jnp.searchsorted(jnp.cumsum(tallies), jnp.arange(rows * top), side="right").astype(jnp.int32)
    listing = labels.reshape(top, rows).T
    listing = listing[jax.random.permutation(jax.random.fold_in(own, 1), rows)]
    offset_by = jax.random.randint(jax.random.fold_in(own, 2), (rows, 1), 0, top)
    return jnp.take_along_axis(listing, (jnp.arange(top)[None, :] + offset_by) % top, axis=1)


def portions_of(amount, total, most, lean, full):
    loads = [(1 << 20) // math.isqrt(standing ** lean) + 1 for standing in range(1, amount + 1)]
    largest = most if full else min(most, max(-(-total // amount), total * loads[0] // sum(loads)))
    least = 1 if total - largest >= amount - 1 else 0
    counts, spare = [largest] + [least] * (amount - 1), total - largest - least * (amount - 1)
    while spare > 0:
        candidates = [i for i in range(1, amount) if counts[i] < largest] or [i for i in range(1, amount) if counts[i] < most]
        mass, remaining = sum([loads[i] for i in candidates]), spare
        for i in candidates:
            addition = min(most - counts[i], max(1, remaining * loads[i] // mass), spare)
            counts[i] = counts[i] + addition
            spare = spare - addition
    return np.array(counts)


def scatter_about(stream_key, dims, spread, most, cuts=(), kind=jnp.bfloat16):
    entries = spread * jax.random.normal(stream_key, dims, jnp.float32)
    if cuts:
        entries = entries * block_scale(stream_key, dims, cuts, -0.22, 0.18)
    return jnp.clip(entries, -most, most).astype(kind)


def setup_inputs(seed: int = 0) -> dict:
    keys = jax.random.split(jax.random.key(seed), 8)
    tokens = scatter_about(keys[0], (REPS, TOKENS, D), 1.0, 6.0, ((0, 16), (1, 16)))
    cotangent = scatter_about(keys[1], (REPS, TOKENS, D), 1.0, 6.0, ((0, 16), (1, 16)))
    routes_keys = jax.random.split(jax.random.fold_in(keys[2], 1), REPS * TOKENS // TOK_DEV)
    routes_turns = jax.random.permutation(jax.random.fold_in(keys[2], 3), REPS * TOKENS // TOK_DEV)
    routes = jax.vmap(lambda own, number: routed_block(jax.random.fold_in(keys[2], 2), own, number, TOK_DEV, EXPERTS, TOP, CAP, 2))(routes_keys, routes_turns).reshape((REPS, TOKENS, TOP))
    route_weights = jnp.clip(jnp.exp(math.log(0.5) - 2.3025851 * jax.random.uniform(keys[3], (REPS, TOKENS, TOP), jnp.float32) ** block_scale(keys[3], (REPS, TOKENS, TOP), ((0, 16), (1, 16)), -0.2, 0.2)), 0.05, 0.5)
    gate_weight = scatter_about(keys[4], (REPS, EXPERTS, D, FF), 1.0, 6.0, ((0, 16), (1, 16)))
    up_weight = scatter_about(keys[5], (REPS, EXPERTS, D, FF), 1.0, 6.0, ((0, 16), (1, 16)))
    down_weight = scatter_about(keys[6], (REPS, EXPERTS, FF, D), 1.0, 6.0, ((0, 16), (1, 16)))
    return {"tokens": tokens, "cotangent": cotangent, "routes": routes, "route_weights": route_weights, "gate_weight": gate_weight, "up_weight": up_weight, "down_weight": down_weight}


learn_rate = 2.0


def expert_update(token_rows, cotangent_rows, gate_matrix, up_matrix, down_matrix):
    width_scale = D ** -0.5
    down_scale = FF ** -0.5
    gate_pre = jnp.dot(token_rows, gate_matrix, preferred_element_type=jnp.float32) * width_scale
    up_pre = jnp.dot(token_rows, up_matrix, preferred_element_type=jnp.float32) * width_scale
    sigmoid_gate = jax.nn.sigmoid(gate_pre)
    silu_gate = gate_pre * sigmoid_gate
    hidden = (silu_gate * up_pre).astype(jnp.bfloat16)
    hidden_grad = jnp.dot(cotangent_rows, down_matrix.T, preferred_element_type=jnp.float32) * down_scale
    gate_rows = (hidden_grad * up_pre * sigmoid_gate * (1.0 + gate_pre * (1.0 - sigmoid_gate))).astype(jnp.bfloat16)
    up_rows = (hidden_grad * silu_gate).astype(jnp.bfloat16)
    down_grad = jnp.dot(hidden.T, cotangent_rows, preferred_element_type=jnp.float32) * down_scale
    gate_grad = jnp.dot(token_rows.T, gate_rows, preferred_element_type=jnp.float32) * width_scale
    up_grad = jnp.dot(token_rows.T, up_rows, preferred_element_type=jnp.float32) * width_scale
    new_gate = (gate_matrix.astype(jnp.float32) - learn_rate * gate_grad).astype(jnp.bfloat16)
    new_up = (up_matrix.astype(jnp.float32) - learn_rate * up_grad).astype(jnp.bfloat16)
    new_down = (down_matrix.astype(jnp.float32) - learn_rate * down_grad).astype(jnp.bfloat16)
    return new_gate, new_up, new_down


def group_update(group_args):
    group_tokens, group_cotangent, group_routes, group_weights, gate_all, up_all, down_all = group_args

    def one_expert(expert_args):
        expert, gate_matrix, up_matrix, down_matrix = expert_args
        hits = group_routes == expert
        marked = jnp.any(hits, axis=1).astype(jnp.int32)
        weight = jnp.sum(jnp.where(hits, group_weights, jnp.zeros_like(group_weights)), axis=1)
        order = jnp.argsort(1 - marked, stable=True)[: N_EXP * CAP]
        token_rows = group_tokens[order]
        cotangent_rows = (group_cotangent[order].astype(jnp.float32) * weight[order][:, None]).astype(jnp.bfloat16)
        return expert_update(token_rows, cotangent_rows, gate_matrix, up_matrix, down_matrix)

    return lax.map(one_expert, (jnp.arange(EXPERTS, dtype=jnp.int32), gate_all, up_all, down_all))


def reference(tokens, cotangent, routes, route_weights, gate_weight, up_weight, down_weight):
    new_gate, new_up, new_down = lax.map(group_update, (tokens, cotangent, routes, route_weights, gate_weight, up_weight, down_weight))
    replica = jnp.arange(REPS, dtype=jnp.int32)
    partner = jnp.bitwise_xor(replica, 1 << ROUND)
    side = jnp.bitwise_and(jnp.right_shift(replica, ROUND), 1)

    def mix(updated):
        half = updated.shape[2] // 2
        split = updated.reshape(REPS, EXPERTS, 2, half, updated.shape[3])
        kept = split[replica, :, side]
        received = split[partner, :, side]
        return (0.5 * (kept.astype(jnp.float32) + received.astype(jnp.float32))).astype(jnp.bfloat16)

    return mix(new_gate), mix(new_up), mix(new_down)
```

```python
import jax
import jax.numpy as jnp
from jax import lax
from jax.sharding import PartitionSpec as P

ROUND = 2
LEARN_RATE = 2.0


def exp_route(move):
    route = []
    for i in range(16):
        z, x, c = move(i // 8, (i // 2) % 4, i % 2)
        route.append((i, (z % 2) * 8 + (x % 4) * 2 + c % 2))
    return route


CORE = exp_route(lambda z, x, c: (z, x, c + 1))
FAR_Z = exp_route(lambda z, x, c: (z + 1, x, c))
X_UP = exp_route(lambda z, x, c: (z, x + 1, c))
X_DOWN = exp_route(lambda z, x, c: (z, x - 1, c))
PARTNER = [(r, r ^ (1 << ROUND)) for r in range(16)]


def move(block, route):
    return lax.ppermute(block, "exp", route)


def after(block, *deps):
    return lax.optimization_barrier((block,) + deps)[0]


def sources():
    me = lax.axis_index("exp")
    z, x, c = me // 8, (me // 2) % 4, me % 2

    def of(dz, dx, dc):
        return ((z + dz) % 2) * 8 + ((x + dx) % 4) * 2 + (c + dc) % 2

    return of


def gather_rows(own, far, start):
    left, right = move(after(own, start), X_UP), move(after(own, start), X_DOWN)
    left_far, right_far = move(after(far, left, right), X_UP), move(after(far, left, right), X_DOWN)
    half = own.shape[0] // 2
    up = jnp.concatenate([left[:half], left_far[:half]], 0)
    down = jnp.concatenate([right[half:], right_far[half:]], 0)
    opp_up, opp_down = move(up, X_UP), move(down, X_DOWN)
    mine = [own, left, right, far, left_far, right_far, opp_up, opp_down]
    pairs = [piece for block in mine for piece in (block, move(block, CORE))]
    return jnp.concatenate(pairs, 0), opp_up


def row_weights(table):
    of = sources()
    half = table.shape[1] // 2

    def take(dz, dx, dc):
        return lax.dynamic_slice_in_dim(table, of(dz, dx, dc), 1, 0)[0]

    out = []
    for dz, dx in ((0, 0), (0, -1), (0, 1), (1, 0), (1, -1), (1, 1)):
        out += [take(dz, dx, 0), take(dz, dx, 1)]
    near = [take(0, 2, dc) for dc in (0, 1)]
    far = [take(1, 2, dc) for dc in (0, 1)]
    for part in (slice(0, half), slice(half, None)):
        for dc in (0, 1):
            out += [near[dc][part], far[dc][part]]
    return jnp.concatenate(out)


def average(kept, received):
    return (0.5 * (kept.astype(jnp.float32) + received.astype(jnp.float32))).astype(jnp.bfloat16)


def body(tokens, cotangent, routes, route_weights, gate_weight, up_weight, down_weight):
    own_tokens, own_cotangent = tokens[0], cotangent[0]
    gate, up, down = gate_weight[0, 0], up_weight[0, 0], down_weight[0, 0]
    width, hidden_width = gate.shape
    width_scale, down_scale = width ** (-0.5), hidden_width ** (-0.5)
    experts = jnp.arange(16, dtype=jnp.int32)
    hits = routes[0][None] == experts[:, None, None]
    dense = jnp.sum(jnp.where(hits, route_weights[0][None], 0.0), axis=2)
    table = lax.all_gather(dense, "exp", axis=0, tiled=False)
    mine = lax.dynamic_slice_in_dim(table, lax.axis_index("exp"), 1, 1)[:, 0]
    weight = row_weights(mine)

    cols = width // 2
    far_tokens = move(own_tokens, FAR_Z)
    cots = [own_cotangent[:, :cols], own_cotangent[:, cols:]]
    far_cots = [move(after(cots[0], far_tokens), FAR_Z)]
    far_cots.append(move(after(cots[1], far_cots[0]), FAR_Z))

    all_tokens, last = gather_rows(own_tokens, far_tokens, own_tokens)
    gate_pre = jnp.dot(all_tokens, gate, preferred_element_type=jnp.float32) * width_scale
    up_pre = jnp.dot(all_tokens, up, preferred_element_type=jnp.float32) * width_scale
    sigmoid = jax.nn.sigmoid(gate_pre)
    silu = gate_pre * sigmoid
    hidden = (silu * up_pre).astype(jnp.bfloat16)

    side = jnp.bitwise_and(jnp.right_shift(lax.axis_index("rep"), ROUND), 1)

    def half_of(matrix, which):
        half = matrix.shape[0] // 2
        return lax.dynamic_slice_in_dim(matrix, which * half, half, 0)

    def step(matrix, gradient):
        return (matrix.astype(jnp.float32) - LEARN_RATE * gradient).astype(jnp.bfloat16)

    def to_partner(block):
        return lax.ppermute(block, "rep", PARTNER)

    hidden_grad = 0.0
    mixed_down = []
    hid_send, hid_keep = [
        lax.dynamic_slice_in_dim(hidden, w * (hidden_width // 2), hidden_width // 2, 1)
        for w in (1 - side, side)
    ]
    for j in range(2):
        rows, last = gather_rows(cots[j], far_cots[j], last)
        rows = (rows.astype(jnp.float32) * weight[:, None]).astype(jnp.bfloat16)
        down_cols = down[:, j * cols : (j + 1) * cols]
        hidden_grad = hidden_grad + jnp.einsum(
            "rd,fd->rf", rows, down_cols, preferred_element_type=jnp.float32
        )
        new = []
        for hid, w in ((hid_send, 1 - side), (hid_keep, side)):
            grad = jnp.einsum("rf,rd->fd", hid, rows, preferred_element_type=jnp.float32)
            new.append(step(half_of(down_cols, w), grad * down_scale))
        mixed_down.append(average(new[1], to_partner(new[0])))
    hidden_grad = hidden_grad * down_scale
    gate_rows = (hidden_grad * up_pre * sigmoid * (1.0 + gate_pre * (1.0 - sigmoid))).astype(
        jnp.bfloat16
    )
    up_rows = (hidden_grad * silu).astype(jnp.bfloat16)

    tok_send, tok_keep = [
        lax.dynamic_slice_in_dim(all_tokens, w * cols, cols, 1) for w in (1 - side, side)
    ]
    mixed = []
    for matrix, grads in ((gate, gate_rows), (up, up_rows)):
        new = []
        for tok, w in ((tok_send, 1 - side), (tok_keep, side)):
            grad = jnp.einsum("rd,rf->df", tok, grads, preferred_element_type=jnp.float32)
            new.append(step(half_of(matrix, w), grad * width_scale))
        mixed.append(average(new[1], to_partner(new[0])))
    return (mixed[0][None, None], mixed[1][None, None], jnp.concatenate(mixed_down, 1)[None, None])


def solution(mesh):
    rows, matrices = P("rep", "exp", None), P("rep", "exp", None, None)
    return jax.shard_map(
        body,
        mesh=mesh,
        in_specs=(rows,) * 4 + (matrices,) * 3,
        out_specs=(matrices,) * 3,
        check_vma=False,
    )
```

```python
import functools

import jax
import jax.numpy as jnp
from jax import lax
from jax.experimental import pallas as pl
from jax.experimental.pallas import tpu as pltpu
from jax.sharding import PartitionSpec as P

ROUND = 2
LEARN_RATE = 2.0
EXPERTS = 16
TOK = 128
HALF = TOK // 2
WIDTH = 2048
FF = 512
TABLE = 128
ROWS = 2048


def exp_route(move):
    route = []
    for i in range(16):
        z, x, c = move(i // 8, (i // 2) % 4, i % 2)
        route.append((i, (z % 2) * 8 + (x % 4) * 2 + c % 2))
    return route


CORE = exp_route(lambda z, x, c: (z, x, c + 1))
FAR_Z = exp_route(lambda z, x, c: (z + 1, x, c))
X_UP = exp_route(lambda z, x, c: (z, x + 1, c))
X_DOWN = exp_route(lambda z, x, c: (z, x - 1, c))
PARTNER = [(r, r ^ (1 << ROUND)) for r in range(16)]


def move(block, route):
    return lax.ppermute(block, "exp", route)


def after(block, *deps):
    return lax.optimization_barrier((block,) + deps)[0]


def neighbours(block, *deps):
    block = after(block, *deps) if deps else block
    return move(block, X_UP), move(block, X_DOWN)


def forwards(left, right):
    return move(left[:HALF], X_UP), move(right[HALF:], X_DOWN)


def fence(*groups):
    flat = lax.optimization_barrier(tuple(block for group in groups for block in group))
    out, at = [], 0
    for group in groups:
        out.append(list(flat[at : at + len(group)]))
        at += len(group)
    return out


def whole(shape):
    return pl.BlockSpec(shape, lambda i: (0,) * len(shape), pipeline_mode=pl.Buffered(1))


def chunk_call(kernel, base, groups, sides, shapes, into, flops):
    pieces = [piece for group in groups for piece in group]
    places, at = [], 0
    for group in groups:
        places.append(tuple(range(at, at + len(group))))
        at += len(group)
    chunk = sum(piece.shape[0] for piece in groups[0])
    side_specs = [
        pl.BlockSpec(memory_space=pltpu.SMEM) if s.ndim == 1 else whole(s.shape) for s in sides
    ]
    n_in = len(pieces) + len(sides)
    read = sum(p.size for p in pieces) * 2
    return pl.pallas_call(
        functools.partial(kernel, places, len(pieces), len(sides)),
        grid=(len(groups),),
        out_shape=shapes,
        in_specs=[whole(p.shape) for p in pieces]
        + side_specs
        + [pl.BlockSpec(memory_space=pl.ANY)] * len(into),
        out_specs=[pl.BlockSpec((chunk, s.shape[1]), lambda i: (base + i, 0)) for s in shapes],
        input_output_aliases={n_in + i: i for i in range(len(into))},
        compiler_params=pltpu.CompilerParams(vmem_limit_bytes=48 * 2**20),
        cost_estimate=pl.CostEstimate(
            flops=flops * chunk * len(groups), bytes_accessed=2 * read, transcendentals=0
        ),
    )(*pieces, *sides, *into)


def forward_kernel(places, n_pieces, n_sides, *refs):
    gate, up = refs[n_pieces], refs[n_pieces + 1]
    rows_ref, hidden_ref, a_ref, b_ref = refs[-4:]
    for g, place in enumerate(places):

        @pl.when(pl.program_id(0) == g)
        def _():
            for i, at in with_rows(refs, place):
                rows_ref[at, :] = refs[i][...]

    rows = rows_ref[...]
    gate_pre = jnp.dot(rows, gate[...], preferred_element_type=jnp.float32) * WIDTH**-0.5
    up_pre = jnp.dot(rows, up[...], preferred_element_type=jnp.float32) * WIDTH**-0.5
    sigmoid = jax.nn.sigmoid(gate_pre)
    silu = gate_pre * sigmoid
    hidden_ref[...] = (silu * up_pre).astype(jnp.bfloat16)
    a_ref[...] = up_pre * sigmoid * (1.0 + gate_pre * (1.0 - sigmoid))
    b_ref[...] = silu


def with_rows(refs, place):
    low = 0
    for i in place:
        n = refs[i].shape[0]
        yield i, pl.ds(low, n)
        low += n


def forward(base, groups, gate, up, into=()):
    shapes = [
        jax.ShapeDtypeStruct((ROWS, WIDTH), jnp.bfloat16),
        jax.ShapeDtypeStruct((ROWS, FF), jnp.bfloat16),
        jax.ShapeDtypeStruct((ROWS, FF), jnp.float32),
        jax.ShapeDtypeStruct((ROWS, FF), jnp.float32),
    ]
    return chunk_call(
        forward_kernel, base, groups, (gate, up), shapes, into, 4 * WIDTH * FF
    )


def row_weight(table, me):
    lane = lax.broadcasted_iota(jnp.int32, table.shape, 1)
    mine = (lane % EXPERTS == me) & (lane < 3 * EXPERTS)
    return jnp.sum(jnp.where(mine, table.astype(jnp.float32), 0.0), axis=1, keepdims=True)


def weigh_kernel(places, n_pieces, n_sides, *refs):
    me_ref, out = refs[n_pieces], refs[-1]
    for g, place in enumerate(places):

        @pl.when(pl.program_id(0) == g)
        def _():
            for i, at in with_rows(refs, place):
                table = refs[i][:, WIDTH:]
                block = refs[i][:, :WIDTH].astype(jnp.float32)
                out[at, :] = (block * row_weight(table, me_ref[0])).astype(jnp.bfloat16)


def weigh(base, groups, me, into=()):
    shapes = [jax.ShapeDtypeStruct((ROWS, WIDTH), jnp.bfloat16)]
    return chunk_call(weigh_kernel, base, groups, (me,), shapes, into, 4 * WIDTH)


def weight_table(routes, route_weights):
    hits = routes[:, :, None] == jnp.arange(EXPERTS, dtype=jnp.int32)[None, None, :]
    dense = jnp.sum(jnp.where(hits, route_weights[:, :, None], 0.0), axis=1)
    high = lax.reduce_precision(dense, 8, 7)
    rest = dense - high
    middle = lax.reduce_precision(rest, 8, 7)
    low = rest - middle
    table = jnp.concatenate([high, middle, low], axis=1).astype(jnp.bfloat16)
    return jnp.pad(table, ((0, 0), (0, TABLE - 3 * EXPERTS)))


def average(kept, received):
    return (0.5 * (kept.astype(jnp.float32) + received.astype(jnp.float32))).astype(jnp.bfloat16)


def body(tokens, cotangent, routes, route_weights, gate_weight, up_weight, down_weight):
    own_t, own_c = tokens[0], cotangent[0]
    gate, up, down = gate_weight[0, 0], up_weight[0, 0], down_weight[0, 0]
    width_scale, down_scale = WIDTH**-0.5, FF**-0.5
    me = lax.axis_index("exp").astype(jnp.int32)[None]
    side = jnp.bitwise_and(jnp.right_shift(lax.axis_index("rep"), ROUND), 1)

    table = weight_table(routes[0], route_weights[0])
    own_c = jnp.concatenate([own_c, table], 1)
    top, low = slice(None, HALF), slice(HALF, None)

    def swapped(blocks):
        return [move(block, CORE) for block in blocks]

    left_t, right_t = neighbours(own_t)
    far_t = [move(own_t[top], FAR_Z)]
    (near_t, far_t, own_t, own_c) = fence(
        [left_t, right_t], far_t, [own_t], [own_c]
    )
    own_t, own_c = own_t[0], own_c[0]

    near_c = neighbours(own_c)
    far_t.append(move(own_t[low], FAR_Z))
    pair_t = swapped([own_t, *near_t])
    near_c, far_t, pair_t, near_t, own_c = fence(near_c, far_t, pair_t, near_t, [own_c])
    own_c = own_c[0]
    near_rows = [own_t, *near_t]
    kept = forward(0, [near_rows, pair_t], gate, up)

    opp = [move(near_t[0], X_UP), move(near_c[1], X_DOWN)]
    far_c = [move(own_c[top], FAR_Z)]
    pair_c = swapped([own_c, near_c[0]])
    opp, far_c, pair_c, far_t, near_c, own_c = fence(opp, far_c, pair_c, far_t, near_c, [own_c])
    own_c = own_c[0]

    far_t = jnp.concatenate(far_t, 0)
    far_near_t = neighbours(far_t)
    far_c.append(move(own_c[low], FAR_Z))
    pair_c += swapped([near_c[1]])
    opp_pair = swapped([opp[0]])
    far_near_t, far_c, pair_c, opp_pair, far_t, opp, kept = fence(
        far_near_t, far_c, pair_c, opp_pair, [far_t], opp, kept
    )
    far_t = far_t[0]
    weighted = weigh(0, [[own_c, *near_c], pair_c], me)
    kept = forward(6, [[opp[0], opp_pair[0]]], gate, up, kept)

    far_c = jnp.concatenate(far_c, 0)
    far_near_c = neighbours(far_c)
    far_pair_t = swapped([far_t, *far_near_t])
    far_near_c, far_pair_t, far_near_t, far_c, opp, kept, weighted = fence(
        far_near_c, far_pair_t, far_near_t, [far_c], opp, kept, weighted
    )
    far_c = far_c[0]
    kept = forward(2, [[far_t, *far_near_t], far_pair_t], gate, up, kept)

    far_opp = [move(far_near_t[0], X_UP), move(far_near_c[1], X_DOWN)]
    opp_pair += swapped([opp[1]])
    far_pair_c = swapped([far_c, far_near_c[0]])
    far_opp, opp_pair, far_pair_c, far_near_c, kept = fence(
        far_opp, opp_pair, far_pair_c, far_near_c, kept
    )
    far_pair_c += swapped([far_near_c[1]])
    far_opp_pair = swapped(far_opp)
    weighted = weigh(6, [[opp[1], opp_pair[1]]], me, weighted)
    kept = forward(7, [[far_opp[0], far_opp_pair[0]]], gate, up, kept)
    all_tokens, hidden, a, b = kept
    weighted = weigh(2, [[far_c, *far_near_c], far_pair_c], me, weighted)
    (weighted,) = weigh(7, [[far_opp[1], far_opp_pair[1]]], me, weighted)

    def half_of(matrix, which, axis=0):
        half = matrix.shape[axis] // 2
        return lax.dynamic_slice_in_dim(matrix, which * half, half, axis)

    def step(matrix, gradient):
        return (matrix.astype(jnp.float32) - LEARN_RATE * gradient).astype(jnp.bfloat16)

    def to_partner(block):
        return lax.ppermute(block, "rep", PARTNER)

    gots = []

    def send(block):
        block = after(block, gots[-3]) if len(gots) > 2 else block
        gots.append(to_partner(block))

    cols = WIDTH // 2

    def new_down(weighted, which, part):
        at = slice(part * cols, (part + 1) * cols)
        grad = jnp.einsum(
            "rf,rd->fd", half_of(hidden, which, 1), weighted[:, at], preferred_element_type=jnp.float32
        )
        return step(half_of(down[:, at], which), grad * down_scale)

    sent0 = new_down(weighted, 1 - side, 0)
    send(sent0)
    sent1 = new_down(after(weighted, sent0), 1 - side, 1)
    send(sent1)
    hidden_grad = down_scale * jnp.einsum(
        "rd,fd->rf", after(weighted, sent1), down, preferred_element_type=jnp.float32
    )
    gate_rows = (hidden_grad * a).astype(jnp.bfloat16)
    up_rows = (hidden_grad * b).astype(jnp.bfloat16)

    def new_projection(matrix, grad_rows, which, part=None):
        matrix, rows = half_of(matrix, which), half_of(all_tokens, which, 1)
        if part is not None:
            at = slice(part * (WIDTH // 4), (part + 1) * (WIDTH // 4))
            matrix, rows = matrix[at], rows[:, at]
        grad = jnp.einsum("rd,rf->df", rows, grad_rows, preferred_element_type=jnp.float32)
        return step(matrix, grad * width_scale)

    last = gate_rows
    for matrix, grad_rows in ((gate, gate_rows), (up, up_rows)):
        for part in range(2):
            last = new_projection(matrix, after(grad_rows, last), 1 - side, part)
            send(last)
    gate_rows, up_rows, weighted = lax.optimization_barrier(
        (gate_rows, up_rows, weighted, last)
    )[:3]
    kept = lax.optimization_barrier(
        [new_down(weighted, side, part) for part in range(2)]
        + [new_projection(gate, gate_rows, side), new_projection(up, up_rows, side)]
    )
    mixed_down = jnp.concatenate([average(kept[part], gots[part]) for part in range(2)], 1)
    mixed_gate = average(kept[2], jnp.concatenate(gots[2:4], 0))
    mixed_up = average(kept[3], jnp.concatenate(gots[4:], 0))
    return (mixed_gate[None, None], mixed_up[None, None], mixed_down[None, None])


def solution(mesh):
    rows, matrices = P("rep", "exp", None), P("rep", "exp", None, None)
    return jax.shard_map(
        body,
        mesh=mesh,
        in_specs=(rows,) * 4 + (matrices,) * 3,
        out_specs=(matrices,) * 3,
        check_vma=False,
    )
```

```python
import functools

import jax
import jax.numpy as jnp
from jax import lax
from jax.experimental import pallas as pl
from jax.experimental.pallas import tpu as pltpu
from jax.sharding import PartitionSpec as P

ROUND = 2
LEARN_RATE = 2.0
EXPERTS = 16
TOK = 128
WIDTH = 2048
FF = 512
TABLE = 128
ROWS = 2048


def exp_route(move):
    route = []
    for i in range(16):
        z, x, c = move(i // 8, (i // 2) % 4, i % 2)
        route.append((i, (z % 2) * 8 + (x % 4) * 2 + c % 2))
    return route


CORE = exp_route(lambda z, x, c: (z, x, c + 1))
FAR_Z = exp_route(lambda z, x, c: (z + 1, x, c))
X_UP = exp_route(lambda z, x, c: (z, x + 1, c))
X_DOWN = exp_route(lambda z, x, c: (z, x - 1, c))
PARTNER = [(r, r ^ (1 << ROUND)) for r in range(16)]


def move(block, route):
    return lax.ppermute(block, "exp", route)


def after(block, *deps):
    return lax.optimization_barrier((block,) + deps)[0]


def neighbours(block):
    return move(block, X_UP), move(block, X_DOWN)


def fence(*arrays):
    return lax.optimization_barrier(arrays)


def whole(shape):
    return pl.BlockSpec(shape, lambda i: (0,) * len(shape), pipeline_mode=pl.Buffered(1))


HBM = pl.BlockSpec(memory_space=pl.ANY)
PARAMS = pltpu.CompilerParams(vmem_limit_bytes=60 * 2**20)


def chunk_call(kernel, base, groups, sides, shapes, into, flops, n_held):
    pieces = [piece for group in groups for piece in group]
    heights = [[piece.shape[0] for piece in group] for group in groups]
    chunk = sum(heights[0])
    side_specs = [
        pl.BlockSpec(memory_space=pltpu.SMEM) if s.ndim == 1 else whole(s.shape) for s in sides
    ]
    n_in = len(pieces) + len(sides)
    blocked = [pl.BlockSpec((chunk, s.shape[1]), lambda i: (base + i, 0)) for s in shapes[n_held:]]
    return pl.pallas_call(
        functools.partial(kernel, base, heights, len(pieces), len(into)),
        grid=(len(groups),),
        out_shape=shapes,
        in_specs=[HBM] * len(pieces) + side_specs + [HBM] * len(into),
        out_specs=[HBM] * n_held + blocked,
        scratch_shapes=[
            pltpu.VMEM((chunk * len(groups), pieces[0].shape[1]), jnp.bfloat16),
            pltpu.SemaphoreType.DMA((len(pieces),)),
            pltpu.SemaphoreType.DMA((len(groups),)),
        ],
        input_output_aliases={n_in + i: i for i in range(len(into))},
        compiler_params=PARAMS,
        cost_estimate=pl.CostEstimate(
            flops=flops * chunk * len(groups),
            bytes_accessed=4 * sum(p.size for p in pieces),
            transcendentals=0,
        ),
    )(*pieces, *sides, *into)


def fetch(heights, pieces, rows, sems, then=lambda g: None):
    copies, at = [], 0
    for group in heights:
        copies.append([])
        for n in group:
            i = len(sum(copies, []))
            copies[-1].append(
                pltpu.make_async_copy(pieces[i], rows.at[pl.ds(at, n), :], sems.at[i])
            )
            at += n
    step = pl.program_id(0)

    @pl.when(step == 0)
    def _():
        for group in copies:
            for copy in group:
                copy.start()

    for g, group in enumerate(copies):

        @pl.when(step == g)
        def _():
            for copy in group:
                copy.wait()
            then(g)


def forward_kernel(base, heights, n_pieces, n_into, *refs):
    pieces, gate, up = refs[:n_pieces], refs[n_pieces], refs[n_pieces + 1]
    rows_out, hidden_ref, a_ref, b_ref, held, sems, out_sems = refs[n_pieces + 2 + n_into :]
    chunk = sum(heights[0])
    copies = [
        pltpu.make_async_copy(
            held.at[pl.ds(g * chunk, chunk), :],
            rows_out.at[pl.ds((base + g) * chunk, chunk), :],
            out_sems.at[g],
        )
        for g in range(len(heights))
    ]
    fetch(heights, pieces, held, sems, lambda g: copies[g].start())
    step = pl.program_id(0)
    rows = held[pl.ds(pl.multiple_of(step * chunk, chunk), chunk), :]
    gate_pre = jnp.dot(rows, gate[...], preferred_element_type=jnp.float32) * WIDTH**-0.5
    up_pre = jnp.dot(rows, up[...], preferred_element_type=jnp.float32) * WIDTH**-0.5
    sigmoid = jax.nn.sigmoid(gate_pre)
    silu = gate_pre * sigmoid
    hidden_ref[...] = (silu * up_pre).astype(jnp.bfloat16)
    a_ref[...] = up_pre * sigmoid * (1.0 + gate_pre * (1.0 - sigmoid))
    b_ref[...] = silu

    @pl.when(step == len(heights) - 1)
    def _():
        for copy in copies:
            copy.wait()


def forward(base, groups, gate, up, into=()):
    shapes = [
        jax.ShapeDtypeStruct((ROWS, WIDTH), jnp.bfloat16),
        jax.ShapeDtypeStruct((ROWS, FF), jnp.bfloat16),
        jax.ShapeDtypeStruct((ROWS, FF), jnp.float32),
        jax.ShapeDtypeStruct((ROWS, FF), jnp.float32),
    ]
    return chunk_call(
        forward_kernel, base, groups, (gate, up), shapes, into, 4 * WIDTH * FF, 1
    )


def row_weight(table, me):
    lane = lax.broadcasted_iota(jnp.int32, table.shape, 1)
    mine = (lane % EXPERTS == me) & (lane < 3 * EXPERTS)
    return jnp.sum(jnp.where(mine, table.astype(jnp.float32), 0.0), axis=1, keepdims=True)


def weigh_kernel(base, heights, n_pieces, n_into, *refs):
    pieces, me_ref = refs[:n_pieces], refs[n_pieces]
    out, held, sems, _ = refs[n_pieces + 1 + n_into :]
    chunk = sum(heights[0])
    fetch(heights, pieces, held, sems)
    at = pl.ds(pl.multiple_of(pl.program_id(0) * chunk, chunk), chunk)
    weight = row_weight(held[at, WIDTH:], me_ref[0])
    out[...] = (held[at, :WIDTH].astype(jnp.float32) * weight).astype(jnp.bfloat16)


def weigh(base, groups, me, into=()):
    shapes = [jax.ShapeDtypeStruct((ROWS, WIDTH), jnp.bfloat16)]
    return chunk_call(weigh_kernel, base, groups, (me,), shapes, into, 4 * WIDTH, 0)


def label_kernel(cotangent_ref, routes_ref, weights_ref, own_ref):
    row = lax.broadcasted_iota(jnp.int32, (TABLE, TOK), 0)
    dense = jnp.zeros((TABLE, TOK), jnp.float32)
    for j in range(routes_ref.shape[0]):
        hit = routes_ref[j : j + 1, :] == row % EXPERTS
        dense += jnp.where(hit, weights_ref[j : j + 1, :], 0.0)
    high = dense.astype(jnp.bfloat16).astype(jnp.float32)
    middle = (dense - high).astype(jnp.bfloat16).astype(jnp.float32)
    low = (dense - high) - middle
    part = row // EXPERTS
    table = jnp.where(part == 0, high, jnp.where(part == 1, middle, low))
    own_ref[:, :WIDTH] = cotangent_ref[...]
    own_ref[:, WIDTH:] = jnp.where(part < 3, table, 0.0).T.astype(jnp.bfloat16)


def label(cotangent, routes, route_weights):
    return pl.pallas_call(
        label_kernel,
        out_shape=jax.ShapeDtypeStruct((TOK, WIDTH + TABLE), jnp.bfloat16),
        cost_estimate=pl.CostEstimate(flops=2**20, bytes_accessed=2**20, transcendentals=0),
    )(cotangent, routes.T, route_weights.T)


def pack_kernel(heights, *refs):
    n_pieces = len(heights)
    pieces, (out, held, sems, out_sems) = refs[:n_pieces], refs[n_pieces:]
    copies, at = [], 0
    for i, n in enumerate(heights):
        rows = pl.ds(at, n)
        copies.append(
            (
                pltpu.make_async_copy(pieces[i], held.at[rows, :], sems.at[i]),
                pltpu.make_async_copy(held.at[rows, :], out.at[rows, :], out_sems.at[i]),
            )
        )
        at += n
    for arrive, _ in copies:
        arrive.start()
    for arrive, leave in copies:
        arrive.wait()
        leave.start()
    for _, leave in copies:
        leave.wait()


def pack(pieces):
    heights = [piece.shape[0] for piece in pieces]
    shape = (sum(heights), pieces[0].shape[1])
    return pl.pallas_call(
        functools.partial(pack_kernel, heights),
        out_shape=jax.ShapeDtypeStruct(shape, jnp.bfloat16),
        in_specs=[HBM] * len(pieces),
        out_specs=HBM,
        scratch_shapes=[
            pltpu.VMEM(shape, jnp.bfloat16),
            pltpu.SemaphoreType.DMA((len(pieces),)),
            pltpu.SemaphoreType.DMA((len(pieces),)),
        ],
        compiler_params=PARAMS,
        cost_estimate=pl.CostEstimate(flops=0, bytes_accessed=2**20, transcendentals=0),
    )(*pieces)


def back_kernel(weighted_ref, down_ref, a_ref, b_ref, gate_ref, up_ref):
    hidden_grad = FF**-0.5 * lax.dot_general(
        weighted_ref[...],
        down_ref[...],
        (((1,), (1,)), ((), ())),
        preferred_element_type=jnp.float32,
    )
    gate_ref[...] = (hidden_grad * a_ref[...]).astype(jnp.bfloat16)
    up_ref[...] = (hidden_grad * b_ref[...]).astype(jnp.bfloat16)


def back(weighted, down, a, b):
    chunk = 512
    rows = pl.BlockSpec((chunk, WIDTH), lambda i: (i, 0))
    narrow = pl.BlockSpec((chunk, FF), lambda i: (i, 0))
    return pl.pallas_call(
        back_kernel,
        grid=(ROWS // chunk,),
        out_shape=[jax.ShapeDtypeStruct((ROWS, FF), jnp.bfloat16)] * 2,
        in_specs=[rows, whole(down.shape), narrow, narrow],
        out_specs=[narrow, narrow],
        compiler_params=PARAMS,
        cost_estimate=pl.CostEstimate(flops=2**20, bytes_accessed=2**20, transcendentals=0),
    )(weighted, down, a, b)


def average(kept, received):
    return (0.5 * (kept.astype(jnp.float32) + received.astype(jnp.float32))).astype(jnp.bfloat16)


def body(tokens, cotangent, routes, route_weights, gate_weight, up_weight, down_weight):
    own_t, own_c = tokens[0], cotangent[0]
    gate, up, down = gate_weight[0, 0], up_weight[0, 0], down_weight[0, 0]
    width_scale, down_scale = WIDTH**-0.5, FF**-0.5
    me = lax.axis_index("exp").astype(jnp.int32)[None]
    side = jnp.bitwise_and(jnp.right_shift(lax.axis_index("rep"), ROUND), 1)

    own_c = label(own_c, routes[0], route_weights[0])

    def swap(block):
        return move(block, CORE)

    far_t = move(own_t, FAR_Z)
    left_t, right_t = neighbours(own_t)
    left_c, right_c = neighbours(own_c)
    far_t, left_t, right_t, left_c, right_c, own_c = fence(
        far_t, left_t, right_t, left_c, right_c, own_c
    )

    near_t, near_c = pack([own_t, left_t, right_t]), pack([own_c, left_c, right_c])
    pair_t, pair_c = swap(near_t), swap(near_c)
    far_t, left_t, right_c, near_t, near_c, pair_t, pair_c, own_c = fence(
        far_t, left_t, right_c, near_t, near_c, pair_t, pair_c, own_c
    )

    opp_t, opp_c = move(left_t, X_UP), move(right_c, X_DOWN)
    far_left_t, far_right_t = neighbours(far_t)
    far_c = move(own_c, FAR_Z)
    kept = forward(0, [[near_t], [pair_t]], gate, up)
    weighted = weigh(0, [[near_c], [pair_c]], me)
    opp_t, opp_c, far_left_t, far_right_t, far_c, far_t, weighted, kept = fence(
        opp_t, opp_c, far_left_t, far_right_t, far_c, far_t, weighted, kept
    )

    far_left_c, far_right_c = neighbours(far_c)
    opp_pair_t, opp_pair_c = swap(opp_t), swap(opp_c)
    far_near_t = pack([far_t, far_left_t, far_right_t])
    far_pair_t = swap(far_near_t)
    kept = forward(2, [[far_near_t]], gate, up, kept)
    far_left_c, far_right_c, opp_pair_t, opp_pair_c, far_pair_t, far_left_t, *kept = fence(
        far_left_c, far_right_c, opp_pair_t, opp_pair_c, far_pair_t, far_left_t, *kept
    )

    far_opp_t, far_opp_c = move(far_left_t, X_UP), move(far_right_c, X_DOWN)
    far_near_c = pack([far_c, far_left_c, far_right_c])
    far_pair_c = swap(far_near_c)
    kept = forward(3, [[far_pair_t]], gate, up, kept)
    weighted = weigh(2, [[far_near_c]], me, weighted)
    far_opp_t, far_opp_c, far_pair_c, weighted, *kept = fence(
        far_opp_t, far_opp_c, far_pair_c, *weighted, *kept
    )

    far_opp_pair_t, far_opp_pair_c = swap(far_opp_t), swap(far_opp_c)
    weighted = weigh(3, [[far_pair_c]], me, [weighted])
    last_t = [opp_t, opp_pair_t, far_opp_t, far_opp_pair_t]
    all_tokens, hidden, a, b = forward(3, [last_t], gate, up, kept)
    last_c = [opp_c, opp_pair_c, far_opp_c, far_opp_pair_c]
    (weighted,) = weigh(3, [last_c], me, weighted)

    def half_of(matrix, which, axis=0):
        half = matrix.shape[axis] // 2
        return lax.dynamic_slice_in_dim(matrix, which * half, half, axis)

    def step(matrix, gradient):
        return (matrix.astype(jnp.float32) - LEARN_RATE * gradient).astype(jnp.bfloat16)

    def to_partner(block):
        return lax.ppermute(block, "rep", PARTNER)

    def new_down(which, weighted):
        grad = jnp.einsum(
            "rf,rd->fd", half_of(hidden, which, 1), weighted, preferred_element_type=jnp.float32
        )
        return step(half_of(down, which), grad * down_scale)

    def new_projection(matrix, which, grad_rows):
        grad = jnp.einsum(
            "rd,rf->df",
            half_of(all_tokens, which, 1),
            grad_rows,
            preferred_element_type=jnp.float32,
        )
        return step(half_of(matrix, which), grad * width_scale)

    sent_down = new_down(1 - side, weighted)
    got_down = to_partner(sent_down)
    gate_rows, up_rows = back(after(weighted, sent_down), down, a, b)
    sent_gate = new_projection(gate, 1 - side, gate_rows)
    got_gate = to_partner(sent_gate)
    up_rows, got_down, weighted, _ = lax.optimization_barrier(
        (up_rows, got_down, weighted, sent_gate)
    )
    sent_up = new_projection(up, 1 - side, up_rows)
    got_up = to_partner(sent_up)
    kept_down = after(new_down(side, after(weighted, sent_up)))
    mixed_down = average(kept_down, got_down)
    gate_rows, up_rows, got_gate, mixed_down = lax.optimization_barrier(
        (gate_rows, up_rows, got_gate, mixed_down)
    )
    kept_gate, kept_up = lax.optimization_barrier(
        (new_projection(gate, side, gate_rows), new_projection(up, side, up_rows))
    )
    mixed_gate = average(kept_gate, got_gate)
    mixed_up = average(kept_up, got_up)
    return (mixed_gate[None, None], mixed_up[None, None], mixed_down[None, None])


def solution(mesh):
    rows, matrices = P("rep", "exp", None), P("rep", "exp", None, None)
    return jax.shard_map(
        body,
        mesh=mesh,
        in_specs=(rows,) * 4 + (matrices,) * 3,
        out_specs=(matrices,) * 3,
        check_vma=False,
    )
```

```python
import functools

import jax
import jax.numpy as jnp
from jax import lax
from jax.experimental import pallas as pl
from jax.experimental.pallas import tpu as pltpu
from jax.sharding import PartitionSpec as P

ROUND = 2
LEARN_RATE = 2.0
EXPERTS = 16
TOK = 128
WIDTH = 2048
FF = 512
TABLE = 128
ROWS = 2048


def exp_route(move):
    route = []
    for i in range(16):
        z, x, c = move(i // 8, (i // 2) % 4, i % 2)
        route.append((i, (z % 2) * 8 + (x % 4) * 2 + c % 2))
    return route


CORE = exp_route(lambda z, x, c: (z, x, c + 1))
FAR_Z = exp_route(lambda z, x, c: (z + 1, x, c))
X_UP = exp_route(lambda z, x, c: (z, x + 1, c))
X_DOWN = exp_route(lambda z, x, c: (z, x - 1, c))
PARTNER = [(r, r ^ (1 << ROUND)) for r in range(16)]


def move(block, route):
    return lax.ppermute(block, "exp", route)


def after(block, *deps):
    return lax.optimization_barrier((block,) + deps)[0]


def neighbours(block):
    return move(block, X_UP), move(block, X_DOWN)


def fence(*arrays):
    return lax.optimization_barrier(arrays)


def whole(shape):
    return pl.BlockSpec(shape, lambda i: (0,) * len(shape), pipeline_mode=pl.Buffered(1))


HBM = pl.BlockSpec(memory_space=pl.ANY)
PARAMS = pltpu.CompilerParams(vmem_limit_bytes=60 * 2**20)


def chunk_call(kernel, base, groups, sides, shapes, into, flops, n_held):
    pieces = [piece for group in groups for piece in group]
    heights = [[piece.shape[0] for piece in group] for group in groups]
    chunk = sum(heights[0])
    side_specs = [
        pl.BlockSpec(memory_space=pltpu.SMEM) if s.ndim == 1 else whole(s.shape) for s in sides
    ]
    n_in = len(pieces) + len(sides)
    blocked = [pl.BlockSpec((chunk, s.shape[1]), lambda i: (base + i, 0)) for s in shapes[n_held:]]
    return pl.pallas_call(
        functools.partial(kernel, base, heights, len(pieces), len(into)),
        grid=(len(groups),),
        out_shape=shapes,
        in_specs=[HBM] * len(pieces) + side_specs + [HBM] * len(into),
        out_specs=[HBM] * n_held + blocked,
        scratch_shapes=[
            pltpu.VMEM((chunk * len(groups), pieces[0].shape[1]), jnp.bfloat16),
            pltpu.SemaphoreType.DMA((len(pieces),)),
            pltpu.SemaphoreType.DMA((len(groups),)),
        ],
        input_output_aliases={n_in + i: i for i in range(len(into))},
        compiler_params=PARAMS,
        cost_estimate=pl.CostEstimate(
            flops=flops * chunk * len(groups),
            bytes_accessed=4 * sum(p.size for p in pieces),
            transcendentals=0,
        ),
    )(*pieces, *sides, *into)


def fetch(heights, pieces, rows, sems, then=lambda g: None):
    copies, at = [], 0
    for group in heights:
        copies.append([])
        for n in group:
            i = len(sum(copies, []))
            copies[-1].append(
                pltpu.make_async_copy(pieces[i], rows.at[pl.ds(at, n), :], sems.at[i])
            )
            at += n
    step = pl.program_id(0)

    @pl.when(step == 0)
    def _():
        for group in copies:
            for copy in group:
                copy.start()

    for g, group in enumerate(copies):

        @pl.when(step == g)
        def _():
            for copy in group:
                copy.wait()
            then(g)


def forward_kernel(base, heights, n_pieces, n_into, *refs):
    pieces, gate, up = refs[:n_pieces], refs[n_pieces], refs[n_pieces + 1]
    rows_out, hidden_ref, a_ref, b_ref, held, sems, out_sems = refs[n_pieces + 2 + n_into :]
    chunk = sum(heights[0])
    copies = [
        pltpu.make_async_copy(
            held.at[pl.ds(g * chunk, chunk), :],
            rows_out.at[pl.ds((base + g) * chunk, chunk), :],
            out_sems.at[g],
        )
        for g in range(len(heights))
    ]
    fetch(heights, pieces, held, sems, lambda g: copies[g].start())
    step = pl.program_id(0)
    rows = held[pl.ds(pl.multiple_of(step * chunk, chunk), chunk), :]
    gate_pre = jnp.dot(rows, gate[...], preferred_element_type=jnp.float32) * WIDTH**-0.5
    up_pre = jnp.dot(rows, up[...], preferred_element_type=jnp.float32) * WIDTH**-0.5
    sigmoid = jax.nn.sigmoid(gate_pre)
    silu = gate_pre * sigmoid
    hidden_ref[...] = (silu * up_pre).astype(jnp.bfloat16)
    a_ref[...] = up_pre * sigmoid * (1.0 + gate_pre * (1.0 - sigmoid))
    b_ref[...] = silu

    @pl.when(step == len(heights) - 1)
    def _():
        for copy in copies:
            copy.wait()


def forward(base, groups, gate, up, into=()):
    shapes = [
        jax.ShapeDtypeStruct((ROWS, WIDTH), jnp.bfloat16),
        jax.ShapeDtypeStruct((ROWS, FF), jnp.bfloat16),
        jax.ShapeDtypeStruct((ROWS, FF), jnp.float32),
        jax.ShapeDtypeStruct((ROWS, FF), jnp.float32),
    ]
    return chunk_call(
        forward_kernel, base, groups, (gate, up), shapes, into, 4 * WIDTH * FF, 1
    )


def row_weight(table, me):
    lane = lax.broadcasted_iota(jnp.int32, table.shape, 1)
    mine = (lane % EXPERTS == me) & (lane < 3 * EXPERTS)
    return jnp.sum(jnp.where(mine, table.astype(jnp.float32), 0.0), axis=1, keepdims=True)


def weigh_kernel(base, heights, n_pieces, n_into, *refs):
    pieces, me_ref = refs[:n_pieces], refs[n_pieces]
    out, held, sems, _ = refs[n_pieces + 1 + n_into :]
    chunk = sum(heights[0])
    fetch(heights, pieces, held, sems)
    at = pl.ds(pl.multiple_of(pl.program_id(0) * chunk, chunk), chunk)
    weight = row_weight(held[at, WIDTH:], me_ref[0])
    out[...] = (held[at, :WIDTH].astype(jnp.float32) * weight).astype(jnp.bfloat16)


def weigh(base, groups, me, into=()):
    shapes = [jax.ShapeDtypeStruct((ROWS, WIDTH), jnp.bfloat16)]
    return chunk_call(weigh_kernel, base, groups, (me,), shapes, into, 4 * WIDTH, 0)


def label_kernel(cotangent_ref, routes_ref, weights_ref, own_ref):
    row = lax.broadcasted_iota(jnp.int32, (TABLE, TOK), 0)
    dense = jnp.zeros((TABLE, TOK), jnp.float32)
    for j in range(routes_ref.shape[0]):
        hit = routes_ref[j : j + 1, :] == row % EXPERTS
        dense += jnp.where(hit, weights_ref[j : j + 1, :], 0.0)
    high = dense.astype(jnp.bfloat16).astype(jnp.float32)
    middle = (dense - high).astype(jnp.bfloat16).astype(jnp.float32)
    low = (dense - high) - middle
    part = row // EXPERTS
    table = jnp.where(part == 0, high, jnp.where(part == 1, middle, low))
    own_ref[:, :WIDTH] = cotangent_ref[...]
    own_ref[:, WIDTH:] = jnp.where(part < 3, table, 0.0).T.astype(jnp.bfloat16)


def label(cotangent, routes, route_weights):
    return pl.pallas_call(
        label_kernel,
        out_shape=jax.ShapeDtypeStruct((TOK, WIDTH + TABLE), jnp.bfloat16),
        cost_estimate=pl.CostEstimate(flops=2**20, bytes_accessed=2**20, transcendentals=0),
    )(cotangent, routes.T, route_weights.T)


def sent_down_kernel(which_ref, hidden_ref, weighted_ref, down_ref, out_ref, total):
    step = pl.program_id(0)

    @pl.when(step == 0)
    def _():
        total[...] = jnp.zeros_like(total)

    total[...] += lax.dot_general(
        hidden_ref[...],
        weighted_ref[...],
        (((0,), (0,)), ((), ())),
        preferred_element_type=jnp.float32,
    )

    @pl.when(step == pl.num_programs(0) - 1)
    def _():
        gradient = total[...] * FF**-0.5
        matrix = down_ref[...].astype(jnp.float32)
        out_ref[...] = (matrix - LEARN_RATE * gradient).astype(jnp.bfloat16)


def new_down_half(which, hidden, weighted, down):
    chunk, half = 512, FF // 2
    return pl.pallas_call(
        sent_down_kernel,
        grid_spec=pltpu.PrefetchScalarGridSpec(
            num_scalar_prefetch=1,
            grid=(ROWS // chunk,),
            in_specs=[
                pl.BlockSpec((chunk, half), lambda i, which: (i, which[0])),
                pl.BlockSpec((chunk, WIDTH), lambda i, which: (i, 0)),
                pl.BlockSpec((half, WIDTH), lambda i, which: (which[0], 0)),
            ],
            out_specs=pl.BlockSpec((half, WIDTH), lambda i, which: (0, 0)),
            scratch_shapes=[pltpu.VMEM((half, WIDTH), jnp.float32)],
        ),
        out_shape=jax.ShapeDtypeStruct((half, WIDTH), jnp.bfloat16),
        compiler_params=PARAMS,
        cost_estimate=pl.CostEstimate(flops=2**22, bytes_accessed=2**22, transcendentals=0),
    )(which, hidden, weighted, down)


def back_kernel(weighted_ref, down_ref, a_ref, b_ref, gate_ref, up_ref):
    hidden_grad = FF**-0.5 * lax.dot_general(
        weighted_ref[...],
        down_ref[...],
        (((1,), (1,)), ((), ())),
        preferred_element_type=jnp.float32,
    )
    gate_ref[...] = (hidden_grad * a_ref[...]).astype(jnp.bfloat16)
    up_ref[...] = (hidden_grad * b_ref[...]).astype(jnp.bfloat16)


def back(weighted, down, a, b):
    chunk = 512
    rows = pl.BlockSpec((chunk, WIDTH), lambda i: (i, 0))
    narrow = pl.BlockSpec((chunk, FF), lambda i: (i, 0))
    return pl.pallas_call(
        back_kernel,
        grid=(ROWS // chunk,),
        out_shape=[jax.ShapeDtypeStruct((ROWS, FF), jnp.bfloat16)] * 2,
        in_specs=[rows, whole(down.shape), narrow, narrow],
        out_specs=[narrow, narrow],
        compiler_params=PARAMS,
        cost_estimate=pl.CostEstimate(flops=2**20, bytes_accessed=2**20, transcendentals=0),
    )(weighted, down, a, b)


def average(kept, received):
    return (0.5 * (kept.astype(jnp.float32) + received.astype(jnp.float32))).astype(jnp.bfloat16)


def body(tokens, cotangent, routes, route_weights, gate_weight, up_weight, down_weight):
    own_t, own_c = tokens[0], cotangent[0]
    gate, up, down = gate_weight[0, 0], up_weight[0, 0], down_weight[0, 0]
    width_scale, down_scale = WIDTH**-0.5, FF**-0.5
    me = lax.axis_index("exp").astype(jnp.int32)[None]
    side = jnp.bitwise_and(jnp.right_shift(lax.axis_index("rep"), ROUND), 1)

    own_c = label(own_c, routes[0], route_weights[0])

    def swap(block):
        return move(block, CORE)

    far_t = move(own_t, FAR_Z)
    left_t, right_t = neighbours(own_t)
    left_c, right_c = neighbours(own_c)
    far_t, left_t, right_t, left_c, right_c, own_c = fence(
        far_t, left_t, right_t, left_c, right_c, own_c
    )

    near_t, near_c = [own_t, left_t, right_t], [own_c, left_c, right_c]
    pair_t, pair_c = [swap(p) for p in near_t], [swap(p) for p in near_c]
    pair_t, pair_c, near_t, near_c, far_t = fence(pair_t, pair_c, near_t, near_c, far_t)

    opp_t, opp_c = move(near_t[1], X_UP), move(near_c[2], X_DOWN)
    far_left_t, far_right_t = neighbours(far_t)
    far_c = move(near_c[0], FAR_Z)
    kept = forward(0, [near_t, pair_t], gate, up)
    weighted = weigh(0, [near_c, pair_c], me)
    opp_t, opp_c, far_left_t, far_right_t, far_c, far_t, weighted, kept = fence(
        opp_t, opp_c, far_left_t, far_right_t, far_c, far_t, weighted, kept
    )

    far_left_c, far_right_c = neighbours(far_c)
    far_near_t = [far_t, far_left_t, far_right_t]
    far_pair_t = [swap(p) for p in far_near_t]
    kept = forward(2, [far_near_t], gate, up, kept)
    far_left_c, far_right_c, far_pair_t, far_left_t, far_c, kept = fence(
        far_left_c, far_right_c, far_pair_t, far_left_t, far_c, kept
    )

    far_opp_t, far_opp_c = move(far_left_t, X_UP), move(far_right_c, X_DOWN)
    far_near_c = [far_c, far_left_c, far_right_c]
    far_pair_c = [swap(p) for p in far_near_c]
    kept = forward(3, [far_pair_t], gate, up, kept)
    weighted = weigh(2, [far_near_c], me, weighted)
    far_opp_t, far_opp_c, far_pair_c, opp_t, opp_c, weighted, kept = fence(
        far_opp_t, far_opp_c, far_pair_c, opp_t, opp_c, weighted, kept
    )

    opp_pair_t, far_opp_pair_t = swap(opp_t), swap(far_opp_t)
    opp_pair_c, far_opp_pair_c = swap(opp_c), swap(far_opp_c)
    weighted = weigh(3, [far_pair_c], me, weighted)
    last_t = [[opp_t, opp_pair_t], [far_opp_t, far_opp_pair_t]]
    all_tokens, hidden, a, b = forward(6, last_t, gate, up, kept)
    last_c = [[opp_c, opp_pair_c], [far_opp_c, far_opp_pair_c]]
    (weighted,) = weigh(6, last_c, me, weighted)

    def half_of(matrix, which, axis=0):
        half = matrix.shape[axis] // 2
        return lax.dynamic_slice_in_dim(matrix, which * half, half, axis)

    def step(matrix, gradient):
        return (matrix.astype(jnp.float32) - LEARN_RATE * gradient).astype(jnp.bfloat16)

    def to_partner(block):
        return lax.ppermute(block, "rep", PARTNER)

    def new_down(which, weighted):
        grad = jnp.einsum(
            "rf,rd->fd", half_of(hidden, which, 1), weighted, preferred_element_type=jnp.float32
        )
        return step(half_of(down, which), grad * down_scale)

    def new_projection(matrix, which, grad_rows):
        grad = jnp.einsum(
            "rd,rf->df",
            half_of(all_tokens, which, 1),
            grad_rows,
            preferred_element_type=jnp.float32,
        )
        return step(half_of(matrix, which), grad * width_scale)

    sent_down = new_down_half((1 - side).astype(jnp.int32)[None], hidden, weighted, down)
    got_down = to_partner(sent_down)
    gate_rows, up_rows = back(after(weighted, sent_down), down, a, b)
    sent_gate = new_projection(gate, 1 - side, gate_rows)
    got_gate = to_partner(sent_gate)
    up_rows, got_down, weighted, _ = lax.optimization_barrier(
        (up_rows, got_down, weighted, sent_gate)
    )
    sent_up = new_projection(up, 1 - side, up_rows)
    got_up = to_partner(sent_up)
    kept_down = after(new_down(side, after(weighted, sent_up)))
    mixed_down = average(kept_down, got_down)
    gate_rows, up_rows, got_gate, mixed_down = lax.optimization_barrier(
        (gate_rows, up_rows, got_gate, mixed_down)
    )
    kept_gate, kept_up = lax.optimization_barrier(
        (new_projection(gate, side, gate_rows), new_projection(up, side, up_rows))
    )
    mixed_gate = average(kept_gate, got_gate)
    mixed_up = average(kept_up, got_up)
    return (mixed_gate[None, None], mixed_up[None, None], mixed_down[None, None])


def solution(mesh):
    rows, matrices = P("rep", "exp", None), P("rep", "exp", None, None)
    return jax.shard_map(
        body,
        mesh=mesh,
        in_specs=(rows,) * 4 + (matrices,) * 3,
        out_specs=(matrices,) * 3,
        check_vma=False,
    )
```

```python
import functools

import jax
import jax.numpy as jnp
from jax import lax
from jax.experimental import pallas as pl
from jax.experimental.pallas import tpu as pltpu
from jax.sharding import PartitionSpec as P

ROUND = 2
LEARN_RATE = 2.0
EXPERTS = 16
TOK = 128
WIDTH = 2048
FF = 512
TABLE = 128
ROWS = 2048
EARLY = 1152


def exp_route(move):
    route = []
    for i in range(16):
        z, x, c = move(i // 8, (i // 2) % 4, i % 2)
        route.append((i, (z % 2) * 8 + (x % 4) * 2 + c % 2))
    return route


CORE = exp_route(lambda z, x, c: (z, x, c + 1))
FAR_Z = exp_route(lambda z, x, c: (z + 1, x, c))
X_UP = exp_route(lambda z, x, c: (z, x + 1, c))
X_DOWN = exp_route(lambda z, x, c: (z, x - 1, c))
PARTNER = [(r, r ^ (1 << ROUND)) for r in range(16)]


def move(block, route):
    return lax.ppermute(block, "exp", route)


def after(block, *deps):
    return lax.optimization_barrier((block,) + deps)[0]


def neighbours(block):
    return move(block, X_UP), move(block, X_DOWN)


def fence(*arrays):
    return lax.optimization_barrier(arrays)


def whole(shape):
    return pl.BlockSpec(shape, lambda i: (0,) * len(shape), pipeline_mode=pl.Buffered(1))


HBM = pl.BlockSpec(memory_space=pl.ANY)
PARAMS = pltpu.CompilerParams(vmem_limit_bytes=60 * 2**20)


def chunk_call(kernel, base, groups, sides, shapes, into, flops, n_held):
    pieces = [piece for group in groups for piece in group]
    heights = [[piece.shape[0] for piece in group] for group in groups]
    chunk = sum(heights[0])
    side_specs = [
        pl.BlockSpec(memory_space=pltpu.SMEM) if s.ndim == 1 else whole(s.shape) for s in sides
    ]
    n_in = len(pieces) + len(sides)
    blocked = [pl.BlockSpec((chunk, s.shape[1]), lambda i: (base + i, 0)) for s in shapes[n_held:]]
    return pl.pallas_call(
        functools.partial(kernel, base, heights, len(pieces), len(into)),
        grid=(len(groups),),
        out_shape=shapes,
        in_specs=[HBM] * len(pieces) + side_specs + [HBM] * len(into),
        out_specs=[HBM] * n_held + blocked,
        scratch_shapes=[
            pltpu.VMEM((chunk * len(groups), pieces[0].shape[1]), jnp.bfloat16),
            pltpu.SemaphoreType.DMA((len(pieces),)),
            pltpu.SemaphoreType.DMA((len(groups),)),
        ],
        input_output_aliases={n_in + i: i for i in range(len(into))},
        compiler_params=PARAMS,
        cost_estimate=pl.CostEstimate(
            flops=flops * chunk * len(groups),
            bytes_accessed=4 * sum(p.size for p in pieces),
            transcendentals=0,
        ),
    )(*pieces, *sides, *into)


def fetch(heights, pieces, rows, sems, then=lambda g: None):
    copies, at = [], 0
    for group in heights:
        copies.append([])
        for n in group:
            i = len(sum(copies, []))
            copies[-1].append(
                pltpu.make_async_copy(pieces[i], rows.at[pl.ds(at, n), :], sems.at[i])
            )
            at += n
    step = pl.program_id(0)

    @pl.when(step == 0)
    def _():
        for group in copies:
            for copy in group:
                copy.start()

    for g, group in enumerate(copies):

        @pl.when(step == g)
        def _():
            for copy in group:
                copy.wait()
            then(g)


def forward_kernel(base, heights, n_pieces, n_into, *refs):
    pieces, gate, up = refs[:n_pieces], refs[n_pieces], refs[n_pieces + 1]
    rows_out, hidden_ref, a_ref, b_ref, held, sems, out_sems = refs[n_pieces + 2 + n_into :]
    chunk = sum(heights[0])
    copies = [
        pltpu.make_async_copy(
            held.at[pl.ds(g * chunk, chunk), :],
            rows_out.at[pl.ds((base + g) * chunk, chunk), :],
            out_sems.at[g],
        )
        for g in range(len(heights))
    ]
    fetch(heights, pieces, held, sems, lambda g: copies[g].start())
    step = pl.program_id(0)
    rows = held[pl.ds(pl.multiple_of(step * chunk, chunk), chunk), :]
    gate_pre = jnp.dot(rows, gate[...], preferred_element_type=jnp.float32) * WIDTH**-0.5
    up_pre = jnp.dot(rows, up[...], preferred_element_type=jnp.float32) * WIDTH**-0.5
    sigmoid = jax.nn.sigmoid(gate_pre)
    silu = gate_pre * sigmoid
    hidden_ref[...] = (silu * up_pre).astype(jnp.bfloat16)
    a_ref[...] = up_pre * sigmoid * (1.0 + gate_pre * (1.0 - sigmoid))
    b_ref[...] = silu

    @pl.when(step == len(heights) - 1)
    def _():
        for copy in copies:
            copy.wait()


def forward(base, groups, gate, up, into=()):
    shapes = [
        jax.ShapeDtypeStruct((ROWS, WIDTH), jnp.bfloat16),
        jax.ShapeDtypeStruct((ROWS, FF), jnp.bfloat16),
        jax.ShapeDtypeStruct((ROWS, FF), jnp.float32),
        jax.ShapeDtypeStruct((ROWS, FF), jnp.float32),
    ]
    return chunk_call(
        forward_kernel, base, groups, (gate, up), shapes, into, 4 * WIDTH * FF, 1
    )


def row_weight(table, me):
    lane = lax.broadcasted_iota(jnp.int32, table.shape, 1)
    mine = (lane % EXPERTS == me) & (lane < 3 * EXPERTS)
    return jnp.sum(jnp.where(mine, table.astype(jnp.float32), 0.0), axis=1, keepdims=True)


def weigh_kernel(base, heights, n_pieces, n_into, *refs):
    pieces, me_ref = refs[:n_pieces], refs[n_pieces]
    out, held, sems, _ = refs[n_pieces + 1 + n_into :]
    chunk = sum(heights[0])
    fetch(heights, pieces, held, sems)
    at = pl.ds(pl.multiple_of(pl.program_id(0) * chunk, chunk), chunk)
    weight = row_weight(held[at, WIDTH:], me_ref[0])
    out[...] = (held[at, :WIDTH].astype(jnp.float32) * weight).astype(jnp.bfloat16)


def weigh(base, groups, me, into=()):
    shapes = [jax.ShapeDtypeStruct((ROWS, WIDTH), jnp.bfloat16)]
    return chunk_call(weigh_kernel, base, groups, (me,), shapes, into, 4 * WIDTH, 0)


def label_kernel(cotangent_ref, routes_ref, weights_ref, own_ref):
    row = lax.broadcasted_iota(jnp.int32, (TABLE, TOK), 0)
    dense = jnp.zeros((TABLE, TOK), jnp.float32)
    for j in range(routes_ref.shape[0]):
        hit = routes_ref[j : j + 1, :] == row % EXPERTS
        dense += jnp.where(hit, weights_ref[j : j + 1, :], 0.0)
    high = dense.astype(jnp.bfloat16).astype(jnp.float32)
    middle = (dense - high).astype(jnp.bfloat16).astype(jnp.float32)
    low = (dense - high) - middle
    part = row // EXPERTS
    table = jnp.where(part == 0, high, jnp.where(part == 1, middle, low))
    own_ref[:, :WIDTH] = cotangent_ref[...]
    own_ref[:, WIDTH:] = jnp.where(part < 3, table, 0.0).T.astype(jnp.bfloat16)


def label(cotangent, routes, route_weights):
    return pl.pallas_call(
        label_kernel,
        out_shape=jax.ShapeDtypeStruct((TOK, WIDTH + TABLE), jnp.bfloat16),
        cost_estimate=pl.CostEstimate(flops=2**20, bytes_accessed=2**20, transcendentals=0),
    )(cotangent, routes.T, route_weights.T)


def transposed_dot(left, right):
    return lax.dot_general(
        left, right, (((0,), (0,)), ((), ())), preferred_element_type=jnp.float32
    )


def early_down_kernel(which_ref, hidden_ref, weighted_ref, total_ref):
    @pl.when(pl.program_id(0) == 0)
    def _():
        total_ref[...] = jnp.zeros_like(total_ref)

    total_ref[...] += transposed_dot(hidden_ref[...], weighted_ref[...])


def early_down(which, hidden, weighted):
    chunk, half = EARLY // 3, FF // 2
    return pl.pallas_call(
        early_down_kernel,
        grid_spec=pltpu.PrefetchScalarGridSpec(
            num_scalar_prefetch=1,
            grid=(3,),
            in_specs=[
                pl.BlockSpec((chunk, half), lambda i, which: (i, which[0])),
                pl.BlockSpec((chunk, WIDTH), lambda i, which: (i, 0)),
            ],
            out_specs=pl.BlockSpec((half, WIDTH), lambda i, which: (0, 0)),
        ),
        out_shape=jax.ShapeDtypeStruct((half, WIDTH), jnp.float32),
        compiler_params=PARAMS,
        cost_estimate=pl.CostEstimate(flops=2**22, bytes_accessed=2**22, transcendentals=0),
    )(which, hidden, weighted)


def late_down_kernel(groups, which_ref, me_ref, hidden_ref, total_ref, down_ref, *refs):
    n = sum(groups)
    pieces, (_, out_ref, sent_ref, held, rows, sems, out_sems) = refs[:n], refs[n:]
    copies = [
        pltpu.make_async_copy(piece, held.at[pl.ds(i * TOK, TOK), :], sems.at[i])
        for i, piece in enumerate(pieces)
    ]
    for copy in copies:
        copy.start()
    total = total_ref[...]
    first, leaves = 0, []
    for g, count in enumerate(groups):
        for copy in copies[first : first + count]:
            copy.wait()
        at = pl.ds(first * TOK, count * TOK)
        weight = row_weight(held[at, WIDTH:], me_ref[0])
        rows[at, :] = (held[at, :WIDTH].astype(jnp.float32) * weight).astype(jnp.bfloat16)
        leaves.append(
            pltpu.make_async_copy(
                rows.at[at, :],
                out_ref.at[pl.ds(EARLY + first * TOK, count * TOK), :],
                out_sems.at[g],
            )
        )
        leaves[-1].start()
        total += transposed_dot(
            hidden_ref[pl.ds(EARLY + first * TOK, count * TOK), :], rows[at, :]
        )
        first += count
    matrix = down_ref[...].astype(jnp.float32)
    sent_ref[...] = (matrix - LEARN_RATE * (total * FF**-0.5)).astype(jnp.bfloat16)
    for leave in leaves:
        leave.wait()


def late_down(which, me, hidden, total, down, groups, weighted):
    pieces = [piece for group in groups for piece in group]
    half, count = FF // 2, ROWS - EARLY
    return pl.pallas_call(
        functools.partial(late_down_kernel, [len(group) for group in groups]),
        grid_spec=pltpu.PrefetchScalarGridSpec(
            num_scalar_prefetch=1,
            grid=(1,),
            in_specs=[
                pl.BlockSpec(memory_space=pltpu.SMEM),
                pl.BlockSpec((ROWS, half), lambda i, which: (0, which[0])),
                pl.BlockSpec((half, WIDTH), lambda i, which: (0, 0)),
                pl.BlockSpec((half, WIDTH), lambda i, which: (which[0], 0)),
            ]
            + [HBM] * (len(pieces) + 1),
            out_specs=[HBM, pl.BlockSpec((half, WIDTH), lambda i, which: (0, 0))],
            scratch_shapes=[
                pltpu.VMEM((count, WIDTH + TABLE), jnp.bfloat16),
                pltpu.VMEM((count, WIDTH), jnp.bfloat16),
                pltpu.SemaphoreType.DMA((len(pieces),)),
                pltpu.SemaphoreType.DMA((len(groups),)),
            ],
        ),
        out_shape=[
            jax.ShapeDtypeStruct((ROWS, WIDTH), jnp.bfloat16),
            jax.ShapeDtypeStruct((half, WIDTH), jnp.bfloat16),
        ],
        input_output_aliases={5 + len(pieces): 0},
        compiler_params=PARAMS,
        cost_estimate=pl.CostEstimate(flops=2**22, bytes_accessed=2**22, transcendentals=0),
    )(which, me, hidden, total, down, *pieces, weighted)


def back_kernel(weighted_ref, down_ref, a_ref, b_ref, gate_ref, up_ref):
    hidden_grad = FF**-0.5 * lax.dot_general(
        weighted_ref[...],
        down_ref[...],
        (((1,), (1,)), ((), ())),
        preferred_element_type=jnp.float32,
    )
    gate_ref[...] = (hidden_grad * a_ref[...]).astype(jnp.bfloat16)
    up_ref[...] = (hidden_grad * b_ref[...]).astype(jnp.bfloat16)


def back(weighted, down, a, b):
    chunk = 512
    rows = pl.BlockSpec((chunk, WIDTH), lambda i: (i, 0))
    narrow = pl.BlockSpec((chunk, FF), lambda i: (i, 0))
    return pl.pallas_call(
        back_kernel,
        grid=(ROWS // chunk,),
        out_shape=[jax.ShapeDtypeStruct((ROWS, FF), jnp.bfloat16)] * 2,
        in_specs=[rows, whole(down.shape), narrow, narrow],
        out_specs=[narrow, narrow],
        compiler_params=PARAMS,
        cost_estimate=pl.CostEstimate(flops=2**20, bytes_accessed=2**20, transcendentals=0),
    )(weighted, down, a, b)


def average(kept, received):
    return (0.5 * (kept.astype(jnp.float32) + received.astype(jnp.float32))).astype(jnp.bfloat16)


def body(tokens, cotangent, routes, route_weights, gate_weight, up_weight, down_weight):
    own_t, own_c = tokens[0], cotangent[0]
    gate, up, down = gate_weight[0, 0], up_weight[0, 0], down_weight[0, 0]
    width_scale, down_scale = WIDTH**-0.5, FF**-0.5
    me = lax.axis_index("exp").astype(jnp.int32)[None]
    side = jnp.bitwise_and(jnp.right_shift(lax.axis_index("rep"), ROUND), 1)

    own_c = label(own_c, routes[0], route_weights[0])

    def swap(block):
        return move(block, CORE)

    far_t = move(own_t, FAR_Z)
    left_t, right_t = neighbours(own_t)
    left_c, right_c = neighbours(own_c)
    far_t, left_t, right_t, left_c, right_c, own_c = fence(
        far_t, left_t, right_t, left_c, right_c, own_c
    )

    near_t, near_c = [own_t, left_t, right_t], [own_c, left_c, right_c]
    pair_t, pair_c = [swap(p) for p in near_t], [swap(p) for p in near_c]
    pair_t, pair_c, near_t, near_c, far_t = fence(pair_t, pair_c, near_t, near_c, far_t)

    opp_t, opp_c = move(near_t[1], X_UP), move(near_c[2], X_DOWN)
    far_left_t, far_right_t = neighbours(far_t)
    far_c = move(near_c[0], FAR_Z)
    kept = forward(0, [near_t, pair_t], gate, up)
    weighted = weigh(0, [near_c, pair_c], me)
    opp_t, opp_c, far_left_t, far_right_t, far_c, far_t, weighted, kept = fence(
        opp_t, opp_c, far_left_t, far_right_t, far_c, far_t, weighted, kept
    )

    far_left_c, far_right_c = neighbours(far_c)
    far_near_t = [far_t, far_left_t, far_right_t]
    far_pair_t = [swap(p) for p in far_near_t]
    kept = forward(2, [far_near_t], gate, up, kept)
    far_left_c, far_right_c, far_pair_t, far_left_t, far_c, kept = fence(
        far_left_c, far_right_c, far_pair_t, far_left_t, far_c, kept
    )

    far_opp_t, far_opp_c = move(far_left_t, X_UP), move(far_right_c, X_DOWN)
    far_near_c = [far_c, far_left_c, far_right_c]
    far_pair_c = [swap(p) for p in far_near_c]
    (weighted,) = weigh(2, [far_near_c], me, weighted)
    other = (1 - side).astype(jnp.int32)[None]
    kept, total = fence(kept, early_down(other, kept[1], weighted))
    kept = forward(3, [far_pair_t], gate, up, kept)
    far_opp_t, far_opp_c, far_pair_c, opp_t, opp_c, weighted, kept, total = fence(
        far_opp_t, far_opp_c, far_pair_c, opp_t, opp_c, weighted, kept, total
    )

    opp_pair_t, far_opp_pair_t = swap(opp_t), swap(far_opp_t)
    opp_pair_c, far_opp_pair_c = swap(opp_c), swap(far_opp_c)
    last_t = [[opp_t, opp_pair_t], [far_opp_t, far_opp_pair_t]]
    all_tokens, hidden, a, b = forward(6, last_t, gate, up, kept)
    last_c = [far_pair_c, [opp_c, opp_pair_c], [far_opp_c, far_opp_pair_c]]
    weighted, sent_down = late_down(other, me, hidden, total, down, last_c, weighted)

    def half_of(matrix, which, axis=0):
        half = matrix.shape[axis] // 2
        return lax.dynamic_slice_in_dim(matrix, which * half, half, axis)

    def step(matrix, gradient):
        return (matrix.astype(jnp.float32) - LEARN_RATE * gradient).astype(jnp.bfloat16)

    def to_partner(block):
        return lax.ppermute(block, "rep", PARTNER)

    def new_down(which, weighted):
        grad = jnp.einsum(
            "rf,rd->fd", half_of(hidden, which, 1), weighted, preferred_element_type=jnp.float32
        )
        return step(half_of(down, which), grad * down_scale)

    def new_projection(matrix, which, grad_rows):
        grad = jnp.einsum(
            "rd,rf->df",
            half_of(all_tokens, which, 1),
            grad_rows,
            preferred_element_type=jnp.float32,
        )
        return step(half_of(matrix, which), grad * width_scale)

    got_down = to_partner(sent_down)
    gate_rows, up_rows = back(after(weighted, sent_down), down, a, b)
    sent_gate = new_projection(gate, 1 - side, gate_rows)
    got_gate = to_partner(sent_gate)
    up_rows, got_down, weighted, _ = lax.optimization_barrier(
        (up_rows, got_down, weighted, sent_gate)
    )
    sent_up = new_projection(up, 1 - side, up_rows)
    got_up = to_partner(sent_up)
    kept_down = after(new_down(side, after(weighted, sent_up)))
    mixed_down = average(kept_down, got_down)
    gate_rows, up_rows, got_gate, mixed_down = lax.optimization_barrier(
        (gate_rows, up_rows, got_gate, mixed_down)
    )
    kept_gate, kept_up = lax.optimization_barrier(
        (new_projection(gate, side, gate_rows), new_projection(up, side, up_rows))
    )
    mixed_gate = average(kept_gate, got_gate)
    mixed_up = average(kept_up, got_up)
    return (mixed_gate[None, None], mixed_up[None, None], mixed_down[None, None])


def solution(mesh):
    rows, matrices = P("rep", "exp", None), P("rep", "exp", None, None)
    return jax.shard_map(
        body,
        mesh=mesh,
        in_specs=(rows,) * 4 + (matrices,) * 3,
        out_specs=(matrices,) * 3,
        check_vma=False,
    )
```

```python
import functools

import jax
import jax.numpy as jnp
from jax import lax
from jax.experimental import pallas as pl
from jax.experimental.pallas import tpu as pltpu
from jax.sharding import PartitionSpec as P

ROUND = 2
LEARN_RATE = 2.0
EXPERTS = 16
TOK = 128
WIDTH = 2048
FF = 512
TABLE = 128
ROWS = 2048
EARLY = 1152


def exp_route(move):
    route = []
    for i in range(16):
        z, x, c = move(i // 8, (i // 2) % 4, i % 2)
        route.append((i, (z % 2) * 8 + (x % 4) * 2 + c % 2))
    return route


CORE = exp_route(lambda z, x, c: (z, x, c + 1))
FAR_Z = exp_route(lambda z, x, c: (z + 1, x, c))
X_UP = exp_route(lambda z, x, c: (z, x + 1, c))
X_DOWN = exp_route(lambda z, x, c: (z, x - 1, c))
PARTNER = [(r, r ^ (1 << ROUND)) for r in range(16)]


def move(block, route):
    return lax.ppermute(block, "exp", route)


def after(block, *deps):
    return lax.optimization_barrier((block,) + deps)[0]


def neighbours(block):
    return move(block, X_UP), move(block, X_DOWN)


def fence(*arrays):
    return lax.optimization_barrier(arrays)


def whole(shape):
    return pl.BlockSpec(shape, lambda *_: (0,) * len(shape), pipeline_mode=pl.Buffered(1))


HBM = pl.BlockSpec(memory_space=pl.ANY)
PARAMS = pltpu.CompilerParams(vmem_limit_bytes=64 * 2**20)


def chunk_call(kernel, base, groups, sides, side_specs, shapes, into, flops, n_held, splits):
    pieces = [piece for group in groups for piece in group]
    heights = [[piece.shape[0] for piece in group] for group in groups]
    chunk = sum(heights[0])
    n_in = len(pieces) + len(sides)
    blocked = [
        pl.BlockSpec((chunk, s.shape[1] // splits), lambda n, i: (base + i, n))
        for s in shapes[n_held:]
    ]
    return pl.pallas_call(
        functools.partial(kernel, base, heights, len(pieces), len(into)),
        grid=(splits, len(groups)),
        out_shape=shapes,
        in_specs=[HBM] * len(pieces) + side_specs + [HBM] * len(into),
        out_specs=[HBM] * n_held + blocked,
        scratch_shapes=[
            pltpu.VMEM((chunk * len(groups), pieces[0].shape[1]), jnp.bfloat16),
            pltpu.SemaphoreType.DMA((len(pieces),)),
            pltpu.SemaphoreType.DMA((len(groups),)),
        ],
        input_output_aliases={n_in + i: i for i in range(len(into))},
        compiler_params=PARAMS,
        cost_estimate=pl.CostEstimate(
            flops=flops * chunk * len(groups),
            bytes_accessed=4 * sum(p.size for p in pieces),
            transcendentals=0,
        ),
    )(*pieces, *sides, *into)


def fetch(heights, pieces, rows, sems, then=lambda g: None):
    copies, at = [], 0
    for group in heights:
        copies.append([])
        for n in group:
            i = len(sum(copies, []))
            copies[-1].append(
                pltpu.make_async_copy(pieces[i], rows.at[pl.ds(at, n), :], sems.at[i])
            )
            at += n
    first, step = pl.program_id(0) == 0, pl.program_id(1)

    @pl.when(first & (step == 0))
    def _():
        for group in copies:
            for copy in group:
                copy.start()

    for g, group in enumerate(copies):

        @pl.when(first & (step == g))
        def _():
            for copy in group:
                copy.wait()
            then(g)


def forward_kernel(base, heights, n_pieces, n_into, *refs):
    pieces, gate, up = refs[:n_pieces], refs[n_pieces], refs[n_pieces + 1]
    rows_out, hidden_ref, a_ref, b_ref, held, sems, out_sems = refs[n_pieces + 2 + n_into :]
    chunk = sum(heights[0])
    copies = [
        pltpu.make_async_copy(
            held.at[pl.ds(g * chunk, chunk), :],
            rows_out.at[pl.ds((base + g) * chunk, chunk), :],
            out_sems.at[g],
        )
        for g in range(len(heights))
    ]
    fetch(heights, pieces, held, sems, lambda g: copies[g].start())
    step = pl.program_id(1)
    rows = held[pl.ds(pl.multiple_of(step * chunk, chunk), chunk), :]
    gate_pre = jnp.dot(rows, gate[...], preferred_element_type=jnp.float32) * WIDTH**-0.5
    up_pre = jnp.dot(rows, up[...], preferred_element_type=jnp.float32) * WIDTH**-0.5
    sigmoid = jax.nn.sigmoid(gate_pre)
    silu = gate_pre * sigmoid
    hidden_ref[...] = (silu * up_pre).astype(jnp.bfloat16)
    a_ref[...] = up_pre * sigmoid * (1.0 + gate_pre * (1.0 - sigmoid))
    b_ref[...] = silu

    @pl.when((pl.program_id(0) == pl.num_programs(0) - 1) & (step == len(heights) - 1))
    def _():
        for copy in copies:
            copy.wait()


def forward(base, groups, gate, up, into=()):
    shapes = [
        jax.ShapeDtypeStruct((ROWS, WIDTH), jnp.bfloat16),
        jax.ShapeDtypeStruct((ROWS, FF), jnp.bfloat16),
        jax.ShapeDtypeStruct((ROWS, FF), jnp.float32),
        jax.ShapeDtypeStruct((ROWS, FF), jnp.float32),
    ]
    splits = 2 if len(groups) == 1 else 1
    specs = [pl.BlockSpec((WIDTH, FF // splits), lambda n, i: (0, n))] * 2
    return chunk_call(
        forward_kernel, base, groups, (gate, up), specs, shapes, into, 4 * WIDTH * FF, 1, splits
    )


def row_weight(table, me):
    lane = lax.broadcasted_iota(jnp.int32, table.shape, 1)
    mine = (lane % EXPERTS == me) & (lane < 3 * EXPERTS)
    return jnp.sum(jnp.where(mine, table.astype(jnp.float32), 0.0), axis=1, keepdims=True)


def weigh_kernel(base, heights, n_pieces, n_into, *refs):
    pieces, me_ref = refs[:n_pieces], refs[n_pieces]
    out, held, sems, _ = refs[n_pieces + 1 + n_into :]
    chunk = sum(heights[0])
    fetch(heights, pieces, held, sems)
    at = pl.ds(pl.multiple_of(pl.program_id(1) * chunk, chunk), chunk)
    weight = row_weight(held[at, WIDTH:], me_ref[0])
    out[...] = (held[at, :WIDTH].astype(jnp.float32) * weight).astype(jnp.bfloat16)


def weigh(base, groups, me, into=()):
    shapes = [jax.ShapeDtypeStruct((ROWS, WIDTH), jnp.bfloat16)]
    specs = [pl.BlockSpec(memory_space=pltpu.SMEM)]
    return chunk_call(
        weigh_kernel, base, groups, (me,), specs, shapes, into, 4 * WIDTH, 0, 1
    )


def label_kernel(cotangent_ref, routes_ref, weights_ref, own_ref):
    row = lax.broadcasted_iota(jnp.int32, (TABLE, TOK), 0)
    dense = jnp.zeros((TABLE, TOK), jnp.float32)
    for j in range(routes_ref.shape[0]):
        hit = routes_ref[j : j + 1, :] == row % EXPERTS
        dense += jnp.where(hit, weights_ref[j : j + 1, :], 0.0)
    high = dense.astype(jnp.bfloat16).astype(jnp.float32)
    middle = (dense - high).astype(jnp.bfloat16).astype(jnp.float32)
    low = (dense - high) - middle
    part = row // EXPERTS
    table = jnp.where(part == 0, high, jnp.where(part == 1, middle, low))
    own_ref[:, :WIDTH] = cotangent_ref[...]
    own_ref[:, WIDTH:] = jnp.where(part < 3, table, 0.0).T.astype(jnp.bfloat16)


def label(cotangent, routes, route_weights):
    return pl.pallas_call(
        label_kernel,
        out_shape=jax.ShapeDtypeStruct((TOK, WIDTH + TABLE), jnp.bfloat16),
        cost_estimate=pl.CostEstimate(flops=2**20, bytes_accessed=2**20, transcendentals=0),
    )(cotangent, routes.T, route_weights.T)


def transposed_dot(left, right):
    return lax.dot_general(
        left, right, (((0,), (0,)), ((), ())), preferred_element_type=jnp.float32
    )


def early_down_kernel(which_ref, hidden_ref, weighted_ref, *refs):
    before, total_ref = refs[:-1], refs[-1]

    @pl.when(pl.program_id(0) == 0)
    def _():
        total_ref[...] = before[0][...] if before else jnp.zeros_like(total_ref)

    total_ref[...] += transposed_dot(hidden_ref[...], weighted_ref[...])


def early_down(which, hidden, weighted, first, count, before=()):
    chunk, half = EARLY // 3, FF // 2
    result = pl.BlockSpec((half, WIDTH), lambda i, which: (0, 0))
    return pl.pallas_call(
        early_down_kernel,
        grid_spec=pltpu.PrefetchScalarGridSpec(
            num_scalar_prefetch=1,
            grid=(count,),
            in_specs=[
                pl.BlockSpec((chunk, half), lambda i, which: (first + i, which[0])),
                pl.BlockSpec((chunk, WIDTH), lambda i, which: (first + i, 0)),
            ]
            + [result] * len(before),
            out_specs=result,
        ),
        out_shape=jax.ShapeDtypeStruct((half, WIDTH), jnp.float32),
        compiler_params=PARAMS,
        cost_estimate=pl.CostEstimate(flops=2**22, bytes_accessed=2**22, transcendentals=0),
    )(which, hidden, weighted, *before)


def late_down_kernel(groups, which_ref, me_ref, hidden_ref, total_ref, down_ref, *refs):
    n = sum(groups)
    pieces, (_, out_ref, sent_ref, held, rows, sems, out_sems) = refs[:n], refs[n:]
    copies = [
        pltpu.make_async_copy(piece, held.at[pl.ds(i * TOK, TOK), :], sems.at[i])
        for i, piece in enumerate(pieces)
    ]
    for copy in copies:
        copy.start()
    total = total_ref[...]
    first, leaves = 0, []
    for g, count in enumerate(groups):
        for copy in copies[first : first + count]:
            copy.wait()
        at = pl.ds(first * TOK, count * TOK)
        weight = row_weight(held[at, WIDTH:], me_ref[0])
        rows[at, :] = (held[at, :WIDTH].astype(jnp.float32) * weight).astype(jnp.bfloat16)
        leaves.append(
            pltpu.make_async_copy(
                rows.at[at, :],
                out_ref.at[pl.ds(EARLY + first * TOK, count * TOK), :],
                out_sems.at[g],
            )
        )
        leaves[-1].start()
        total += transposed_dot(
            hidden_ref[pl.ds(EARLY + first * TOK, count * TOK), :], rows[at, :]
        )
        first += count
    matrix = down_ref[...].astype(jnp.float32)
    sent_ref[...] = (matrix - LEARN_RATE * (total * FF**-0.5)).astype(jnp.bfloat16)
    for leave in leaves:
        leave.wait()


def late_down(which, me, hidden, total, down, groups, weighted):
    pieces = [piece for group in groups for piece in group]
    half, count = FF // 2, ROWS - EARLY
    return pl.pallas_call(
        functools.partial(late_down_kernel, [len(group) for group in groups]),
        grid_spec=pltpu.PrefetchScalarGridSpec(
            num_scalar_prefetch=1,
            grid=(1,),
            in_specs=[
                pl.BlockSpec(memory_space=pltpu.SMEM),
                pl.BlockSpec((ROWS, half), lambda i, which: (0, which[0])),
                pl.BlockSpec((half, WIDTH), lambda i, which: (0, 0)),
                pl.BlockSpec((half, WIDTH), lambda i, which: (which[0], 0)),
            ]
            + [HBM] * (len(pieces) + 1),
            out_specs=[HBM, pl.BlockSpec((half, WIDTH), lambda i, which: (0, 0))],
            scratch_shapes=[
                pltpu.VMEM((count, WIDTH + TABLE), jnp.bfloat16),
                pltpu.VMEM((count, WIDTH), jnp.bfloat16),
                pltpu.SemaphoreType.DMA((len(pieces),)),
                pltpu.SemaphoreType.DMA((len(groups),)),
            ],
        ),
        out_shape=[
            jax.ShapeDtypeStruct((ROWS, WIDTH), jnp.bfloat16),
            jax.ShapeDtypeStruct((half, WIDTH), jnp.bfloat16),
        ],
        input_output_aliases={5 + len(pieces): 0},
        compiler_params=PARAMS,
        cost_estimate=pl.CostEstimate(flops=2**22, bytes_accessed=2**22, transcendentals=0),
    )(which, me, hidden, total, down, *pieces, weighted)


def back_kernel(weighted_ref, down_ref, a_ref, b_ref, gate_ref, up_ref):
    hidden_grad = FF**-0.5 * lax.dot_general(
        weighted_ref[...],
        down_ref[...],
        (((1,), (1,)), ((), ())),
        preferred_element_type=jnp.float32,
    )
    gate_ref[...] = (hidden_grad * a_ref[...]).astype(jnp.bfloat16)
    up_ref[...] = (hidden_grad * b_ref[...]).astype(jnp.bfloat16)


def back(weighted, down, a, b):
    chunk = 512
    rows = pl.BlockSpec((chunk, WIDTH), lambda i: (i, 0))
    narrow = pl.BlockSpec((chunk, FF), lambda i: (i, 0))
    return pl.pallas_call(
        back_kernel,
        grid=(ROWS // chunk,),
        out_shape=[jax.ShapeDtypeStruct((ROWS, FF), jnp.bfloat16)] * 2,
        in_specs=[rows, whole(down.shape), narrow, narrow],
        out_specs=[narrow, narrow],
        compiler_params=PARAMS,
        cost_estimate=pl.CostEstimate(flops=2**20, bytes_accessed=2**20, transcendentals=0),
    )(weighted, down, a, b)


def average(kept, received):
    return (0.5 * (kept.astype(jnp.float32) + received.astype(jnp.float32))).astype(jnp.bfloat16)


def body(tokens, cotangent, routes, route_weights, gate_weight, up_weight, down_weight):
    own_t, own_c = tokens[0], cotangent[0]
    gate, up, down = gate_weight[0, 0], up_weight[0, 0], down_weight[0, 0]
    width_scale, down_scale = WIDTH**-0.5, FF**-0.5
    me = lax.axis_index("exp").astype(jnp.int32)[None]
    side = jnp.bitwise_and(jnp.right_shift(lax.axis_index("rep"), ROUND), 1)

    own_c = label(own_c, routes[0], route_weights[0])

    def swap(block):
        return move(block, CORE)

    far_t = move(after(own_t, own_c), FAR_Z)
    left_t, right_t = neighbours(own_t)
    left_c, right_c = neighbours(own_c)
    far_t, left_t, right_t, left_c, right_c, own_c = fence(
        far_t, left_t, right_t, left_c, right_c, own_c
    )

    near_t, near_c = [own_t, left_t, right_t], [own_c, left_c, right_c]
    pair_t, pair_c = [swap(p) for p in near_t], [swap(p) for p in near_c]
    pair_t, pair_c, near_t, near_c, far_t = fence(pair_t, pair_c, near_t, near_c, far_t)

    opp_t, opp_c = move(near_t[1], X_UP), move(near_c[2], X_DOWN)
    far_left_t, far_right_t = neighbours(far_t)
    far_c = move(near_c[0], FAR_Z)
    kept = forward(0, [near_t, pair_t], gate, up)
    weighted = weigh(0, [near_c, pair_c], me)
    opp_t, opp_c, far_left_t, far_right_t, far_c, far_t, weighted, kept = fence(
        opp_t, opp_c, far_left_t, far_right_t, far_c, far_t, weighted, kept
    )

    far_left_c, far_right_c = neighbours(far_c)
    far_near_t = [far_t, far_left_t, far_right_t]
    far_pair_t = [swap(p) for p in far_near_t]
    other = (1 - side).astype(jnp.int32)[None]
    kept, weighted, total = fence(kept, weighted, early_down(other, kept[1], weighted[0], 0, 2))
    kept = forward(2, [far_near_t], gate, up, kept)
    far_left_c, far_right_c, far_pair_t, far_left_t, far_c, kept, weighted, total = fence(
        far_left_c, far_right_c, far_pair_t, far_left_t, far_c, kept, weighted, total
    )

    far_opp_t, far_opp_c = move(far_left_t, X_UP), move(far_right_c, X_DOWN)
    far_near_c = [far_c, far_left_c, far_right_c]
    far_pair_c = [swap(p) for p in far_near_c]
    (weighted,) = weigh(2, [far_near_c], me, weighted)
    kept, total = fence(kept, early_down(other, kept[1], weighted, 2, 1, (total,)))
    kept = forward(3, [far_pair_t], gate, up, kept)
    far_opp_t, far_opp_c, far_pair_c, opp_t, opp_c, weighted, kept, total = fence(
        far_opp_t, far_opp_c, far_pair_c, opp_t, opp_c, weighted, kept, total
    )

    opp_pair_t, far_opp_pair_t = swap(opp_t), swap(far_opp_t)
    opp_pair_c, far_opp_pair_c = swap(opp_c), swap(far_opp_c)
    last_t = [[opp_t, opp_pair_t], [far_opp_t, far_opp_pair_t]]
    all_tokens, hidden, a, b = forward(6, last_t, gate, up, kept)
    last_c = [far_pair_c, [opp_c, opp_pair_c], [far_opp_c, far_opp_pair_c]]
    weighted, sent_down = late_down(other, me, hidden, total, down, last_c, weighted)

    def half_of(matrix, which, axis=0):
        half = matrix.shape[axis] // 2
        return lax.dynamic_slice_in_dim(matrix, which * half, half, axis)

    def step(matrix, gradient):
        return (matrix.astype(jnp.float32) - LEARN_RATE * gradient).astype(jnp.bfloat16)

    def to_partner(block):
        return lax.ppermute(block, "rep", PARTNER)

    def new_down(which, weighted):
        grad = jnp.einsum(
            "rf,rd->fd", half_of(hidden, which, 1), weighted, preferred_element_type=jnp.float32
        )
        return step(half_of(down, which), grad * down_scale)

    def new_projection(matrix, which, grad_rows):
        grad = jnp.einsum(
            "rd,rf->df",
            half_of(all_tokens, which, 1),
            grad_rows,
            preferred_element_type=jnp.float32,
        )
        return step(half_of(matrix, which), grad * width_scale)

    got_down = to_partner(sent_down)
    gate_rows, up_rows = back(after(weighted, sent_down), down, a, b)
    sent_gate = new_projection(gate, 1 - side, gate_rows)
    got_gate = to_partner(sent_gate)
    up_rows, got_down, weighted, _ = lax.optimization_barrier(
        (up_rows, got_down, weighted, sent_gate)
    )
    sent_up = new_projection(up, 1 - side, up_rows)
    got_up = to_partner(sent_up)
    kept_down = after(new_down(side, after(weighted, sent_up)))
    mixed_down = average(kept_down, got_down)
    gate_rows, up_rows, got_gate, mixed_down = lax.optimization_barrier(
        (gate_rows, up_rows, got_gate, mixed_down)
    )
    kept_gate, kept_up = lax.optimization_barrier(
        (new_projection(gate, side, gate_rows), new_projection(up, side, up_rows))
    )
    mixed_gate = average(kept_gate, got_gate)
    mixed_up = average(kept_up, got_up)
    return (mixed_gate[None, None], mixed_up[None, None], mixed_down[None, None])


def solution(mesh):
    rows, matrices = P("rep", "exp", None), P("rep", "exp", None, None)
    return jax.shard_map(
        body,
        mesh=mesh,
        in_specs=(rows,) * 4 + (matrices,) * 3,
        out_specs=(matrices,) * 3,
        check_vma=False,
    )
```

```python
import functools

import jax
import jax.numpy as jnp
from jax import lax
from jax.experimental import pallas as pl
from jax.experimental.pallas import tpu as pltpu
from jax.sharding import PartitionSpec as P

ROUND = 2
LEARN_RATE = 2.0
EXPERTS = 16
TOK = 128
WIDTH = 2048
FF = 512
TABLE = 128
ROWS = 2048
EARLY = 1152


def exp_route(move):
    route = []
    for i in range(16):
        z, x, c = move(i // 8, (i // 2) % 4, i % 2)
        route.append((i, (z % 2) * 8 + (x % 4) * 2 + c % 2))
    return route


CORE = exp_route(lambda z, x, c: (z, x, c + 1))
FAR_Z = exp_route(lambda z, x, c: (z + 1, x, c))
X_UP = exp_route(lambda z, x, c: (z, x + 1, c))
X_DOWN = exp_route(lambda z, x, c: (z, x - 1, c))
PARTNER = [(r, r ^ (1 << ROUND)) for r in range(16)]


def move(block, route):
    return lax.ppermute(block, "exp", route)


def after(block, *deps):
    return lax.optimization_barrier((block,) + deps)[0]


def neighbours(block):
    return move(block, X_UP), move(block, X_DOWN)


def fence(*arrays):
    return lax.optimization_barrier(arrays)


def whole(shape):
    return pl.BlockSpec(shape, lambda *_: (0,) * len(shape), pipeline_mode=pl.Buffered(1))


HBM = pl.BlockSpec(memory_space=pl.ANY)
PARAMS = pltpu.CompilerParams(vmem_limit_bytes=64 * 2**20)


def chunk_call(kernel, base, groups, sides, side_specs, shapes, into, flops, n_held, splits):
    pieces = [piece for group in groups for piece in group]
    heights = [[piece.shape[0] for piece in group] for group in groups]
    chunk = sum(heights[0])
    n_in = len(pieces) + len(sides)
    blocked = [
        pl.BlockSpec((chunk, s.shape[1] // splits), lambda n, i: (base + i, n))
        for s in shapes[n_held:]
    ]
    return pl.pallas_call(
        functools.partial(kernel, base, heights, len(pieces), len(into)),
        grid=(splits, len(groups)),
        out_shape=shapes,
        in_specs=[HBM] * len(pieces) + side_specs + [HBM] * len(into),
        out_specs=[HBM] * n_held + blocked,
        scratch_shapes=[
            pltpu.VMEM((chunk * len(groups), pieces[0].shape[1]), jnp.bfloat16),
            pltpu.SemaphoreType.DMA((len(pieces),)),
            pltpu.SemaphoreType.DMA((len(groups),)),
        ],
        input_output_aliases={n_in + i: i for i in range(len(into))},
        compiler_params=PARAMS,
        cost_estimate=pl.CostEstimate(
            flops=flops * chunk * len(groups),
            bytes_accessed=4 * sum(p.size for p in pieces),
            transcendentals=0,
        ),
    )(*pieces, *sides, *into)


def fetch(heights, pieces, rows, sems, then=lambda g: None):
    copies, at = [], 0
    for group in heights:
        copies.append([])
        for n in group:
            i = len(sum(copies, []))
            copies[-1].append(
                pltpu.make_async_copy(pieces[i], rows.at[pl.ds(at, n), :], sems.at[i])
            )
            at += n
    first, step = pl.program_id(0) == 0, pl.program_id(1)

    @pl.when(first & (step == 0))
    def _():
        for group in copies:
            for copy in group:
                copy.start()

    for g, group in enumerate(copies):

        @pl.when(first & (step == g))
        def _():
            for copy in group:
                copy.wait()
            then(g)


def forward_kernel(base, heights, n_pieces, n_into, *refs):
    pieces, gate, up = refs[:n_pieces], refs[n_pieces], refs[n_pieces + 1]
    rows_out, hidden_ref, a_ref, b_ref, held, sems, out_sems = refs[n_pieces + 2 + n_into :]
    chunk = sum(heights[0])
    copies = [
        pltpu.make_async_copy(
            held.at[pl.ds(g * chunk, chunk), :],
            rows_out.at[pl.ds((base + g) * chunk, chunk), :],
            out_sems.at[g],
        )
        for g in range(len(heights))
    ]
    fetch(heights, pieces, held, sems, lambda g: copies[g].start())
    step = pl.program_id(1)
    rows = held[pl.ds(pl.multiple_of(step * chunk, chunk), chunk), :]
    gate_pre = jnp.dot(rows, gate[...], preferred_element_type=jnp.float32) * WIDTH**-0.5
    up_pre = jnp.dot(rows, up[...], preferred_element_type=jnp.float32) * WIDTH**-0.5
    sigmoid = jax.nn.sigmoid(gate_pre)
    silu = gate_pre * sigmoid
    hidden_ref[...] = (silu * up_pre).astype(jnp.bfloat16)
    a_ref[...] = up_pre * sigmoid * (1.0 + gate_pre * (1.0 - sigmoid))
    b_ref[...] = silu

    @pl.when((pl.program_id(0) == pl.num_programs(0) - 1) & (step == len(heights) - 1))
    def _():
        for copy in copies:
            copy.wait()


def forward(base, groups, gate, up, into=()):
    shapes = [
        jax.ShapeDtypeStruct((ROWS, WIDTH), jnp.bfloat16),
        jax.ShapeDtypeStruct((ROWS, FF), jnp.bfloat16),
        jax.ShapeDtypeStruct((ROWS, FF), jnp.float32),
        jax.ShapeDtypeStruct((ROWS, FF), jnp.float32),
    ]
    splits = 2 if len(groups) == 1 else 1
    specs = [pl.BlockSpec((WIDTH, FF // splits), lambda n, i: (0, n))] * 2
    return chunk_call(
        forward_kernel, base, groups, (gate, up), specs, shapes, into, 4 * WIDTH * FF, 1, splits
    )


def row_weight(table, me):
    lane = lax.broadcasted_iota(jnp.int32, table.shape, 1)
    mine = (lane % EXPERTS == me) & (lane < 3 * EXPERTS)
    return jnp.sum(jnp.where(mine, table.astype(jnp.float32), 0.0), axis=1, keepdims=True)


def weigh_kernel(base, heights, n_pieces, n_into, *refs):
    pieces, me_ref = refs[:n_pieces], refs[n_pieces]
    out, held, sems, _ = refs[n_pieces + 1 + n_into :]
    chunk = sum(heights[0])
    fetch(heights, pieces, held, sems)
    at = pl.ds(pl.multiple_of(pl.program_id(1) * chunk, chunk), chunk)
    weight = row_weight(held[at, WIDTH:], me_ref[0])
    out[...] = (held[at, :WIDTH].astype(jnp.float32) * weight).astype(jnp.bfloat16)


def weigh(base, groups, me, into=()):
    shapes = [jax.ShapeDtypeStruct((ROWS, WIDTH), jnp.bfloat16)]
    specs = [pl.BlockSpec(memory_space=pltpu.SMEM)]
    return chunk_call(
        weigh_kernel, base, groups, (me,), specs, shapes, into, 4 * WIDTH, 0, 1
    )


def label_kernel(cotangent_ref, routes_ref, weights_ref, own_ref):
    row = lax.broadcasted_iota(jnp.int32, (TABLE, TOK), 0)
    dense = jnp.zeros((TABLE, TOK), jnp.float32)
    for j in range(routes_ref.shape[0]):
        hit = routes_ref[j : j + 1, :] == row % EXPERTS
        dense += jnp.where(hit, weights_ref[j : j + 1, :], 0.0)
    high = dense.astype(jnp.bfloat16).astype(jnp.float32)
    middle = (dense - high).astype(jnp.bfloat16).astype(jnp.float32)
    low = (dense - high) - middle
    part = row // EXPERTS
    table = jnp.where(part == 0, high, jnp.where(part == 1, middle, low))
    own_ref[:, :WIDTH] = cotangent_ref[...]
    own_ref[:, WIDTH:] = jnp.where(part < 3, table, 0.0).T.astype(jnp.bfloat16)


def label(cotangent, routes, route_weights):
    return pl.pallas_call(
        label_kernel,
        out_shape=jax.ShapeDtypeStruct((TOK, WIDTH + TABLE), jnp.bfloat16),
        cost_estimate=pl.CostEstimate(flops=2**20, bytes_accessed=2**20, transcendentals=0),
    )(cotangent, routes.T, route_weights.T)


def transposed_dot(left, right):
    return lax.dot_general(
        left, right, (((0,), (0,)), ((), ())), preferred_element_type=jnp.float32
    )


def early_down_kernel(which_ref, hidden_ref, weighted_ref, *refs):
    before, total_ref = refs[:-1], refs[-1]

    @pl.when(pl.program_id(0) == 0)
    def _():
        total_ref[...] = before[0][...] if before else jnp.zeros_like(total_ref)

    total_ref[...] += transposed_dot(hidden_ref[...], weighted_ref[...])


def early_down(which, hidden, weighted, first, count, before=()):
    chunk, half = EARLY // 3, FF // 2
    result = pl.BlockSpec((half, WIDTH), lambda i, which: (0, 0))
    return pl.pallas_call(
        early_down_kernel,
        grid_spec=pltpu.PrefetchScalarGridSpec(
            num_scalar_prefetch=1,
            grid=(count,),
            in_specs=[
                pl.BlockSpec((chunk, half), lambda i, which: (first + i, which[0])),
                pl.BlockSpec((chunk, WIDTH), lambda i, which: (first + i, 0)),
            ]
            + [result] * len(before),
            out_specs=result,
        ),
        out_shape=jax.ShapeDtypeStruct((half, WIDTH), jnp.float32),
        compiler_params=PARAMS,
        cost_estimate=pl.CostEstimate(flops=2**22, bytes_accessed=2**22, transcendentals=0),
    )(which, hidden, weighted, *before)


def late_down_kernel(groups, which_ref, me_ref, hidden_ref, total_ref, down_ref, *refs):
    n = sum(groups)
    pieces, rest = refs[:n], refs[n:]
    _, out_ref, sent_ref, held, rows, hidden, before, matrix, sems, out_sems, side_sems = rest
    half = FF // 2
    at = pl.ds(pl.multiple_of(which_ref[0] * half, half), half)
    sides = [
        pltpu.make_async_copy(hidden_ref.at[pl.ds(EARLY, ROWS - EARLY), at], hidden, side_sems.at[0]),
        pltpu.make_async_copy(total_ref, before, side_sems.at[1]),
        pltpu.make_async_copy(down_ref.at[at, :], matrix, side_sems.at[2]),
    ]
    copies = [
        pltpu.make_async_copy(piece, held.at[pl.ds(i * TOK, TOK), :], sems.at[i])
        for i, piece in enumerate(pieces)
    ]
    for copy in copies + sides:
        copy.start()
    total, first, leaves = None, 0, []
    for g, count in enumerate(groups):
        for copy in copies[first : first + count]:
            copy.wait()
        at = pl.ds(first * TOK, count * TOK)
        weight = row_weight(held[at, WIDTH:], me_ref[0])
        rows[at, :] = (held[at, :WIDTH].astype(jnp.float32) * weight).astype(jnp.bfloat16)
        leaves.append(
            pltpu.make_async_copy(
                rows.at[at, :],
                out_ref.at[pl.ds(EARLY + first * TOK, count * TOK), :],
                out_sems.at[g],
            )
        )
        leaves[-1].start()
        if total is None:
            sides[0].wait()
            sides[1].wait()
            total = before[...]
        total += transposed_dot(hidden[at, :], rows[at, :])
        first += count
    sides[2].wait()
    old = matrix[...].astype(jnp.float32)
    sent_ref[...] = (old - LEARN_RATE * (total * FF**-0.5)).astype(jnp.bfloat16)
    for leave in leaves:
        leave.wait()


def late_down(which, me, hidden, total, down, groups, weighted):
    pieces = [piece for group in groups for piece in group]
    half, count = FF // 2, ROWS - EARLY
    return pl.pallas_call(
        functools.partial(late_down_kernel, [len(group) for group in groups]),
        grid_spec=pltpu.PrefetchScalarGridSpec(
            num_scalar_prefetch=1,
            grid=(1,),
            in_specs=[
                pl.BlockSpec(memory_space=pltpu.SMEM),
            ]
            + [HBM] * (len(pieces) + 4),
            out_specs=[HBM, pl.BlockSpec((half, WIDTH), lambda i, which: (0, 0))],
            scratch_shapes=[
                pltpu.VMEM((count, WIDTH + TABLE), jnp.bfloat16),
                pltpu.VMEM((count, WIDTH), jnp.bfloat16),
                pltpu.VMEM((count, half), jnp.bfloat16),
                pltpu.VMEM((half, WIDTH), jnp.float32),
                pltpu.VMEM((half, WIDTH), jnp.bfloat16),
                pltpu.SemaphoreType.DMA((len(pieces),)),
                pltpu.SemaphoreType.DMA((len(groups),)),
                pltpu.SemaphoreType.DMA((3,)),
            ],
        ),
        out_shape=[
            jax.ShapeDtypeStruct((ROWS, WIDTH), jnp.bfloat16),
            jax.ShapeDtypeStruct((half, WIDTH), jnp.bfloat16),
        ],
        input_output_aliases={5 + len(pieces): 0},
        compiler_params=PARAMS,
        cost_estimate=pl.CostEstimate(flops=2**22, bytes_accessed=2**22, transcendentals=0),
    )(which, me, hidden, total, down, *pieces, weighted)


def back_kernel(weighted_ref, down_ref, a_ref, b_ref, gate_ref, up_ref):
    hidden_grad = FF**-0.5 * lax.dot_general(
        weighted_ref[...],
        down_ref[...],
        (((1,), (1,)), ((), ())),
        preferred_element_type=jnp.float32,
    )
    gate_ref[...] = (hidden_grad * a_ref[...]).astype(jnp.bfloat16)
    up_ref[...] = (hidden_grad * b_ref[...]).astype(jnp.bfloat16)


def back(weighted, down, a, b):
    chunk = 512
    rows = pl.BlockSpec((chunk, WIDTH), lambda i: (i, 0))
    narrow = pl.BlockSpec((chunk, FF), lambda i: (i, 0))
    return pl.pallas_call(
        back_kernel,
        grid=(ROWS // chunk,),
        out_shape=[jax.ShapeDtypeStruct((ROWS, FF), jnp.bfloat16)] * 2,
        in_specs=[rows, whole(down.shape), narrow, narrow],
        out_specs=[narrow, narrow],
        compiler_params=PARAMS,
        cost_estimate=pl.CostEstimate(flops=2**20, bytes_accessed=2**20, transcendentals=0),
    )(weighted, down, a, b)


def average(kept, received):
    return (0.5 * (kept.astype(jnp.float32) + received.astype(jnp.float32))).astype(jnp.bfloat16)


def body(tokens, cotangent, routes, route_weights, gate_weight, up_weight, down_weight):
    own_t, own_c = tokens[0], cotangent[0]
    gate, up, down = gate_weight[0, 0], up_weight[0, 0], down_weight[0, 0]
    width_scale, down_scale = WIDTH**-0.5, FF**-0.5
    me = lax.axis_index("exp").astype(jnp.int32)[None]
    side = jnp.bitwise_and(jnp.right_shift(lax.axis_index("rep"), ROUND), 1)

    own_c = label(own_c, routes[0], route_weights[0])

    def swap(block):
        return move(block, CORE)

    far_t = move(after(own_t, own_c), FAR_Z)
    left_t, right_t = neighbours(own_t)
    left_c, right_c = neighbours(own_c)
    far_t, left_t, right_t, left_c, right_c, own_c = fence(
        far_t, left_t, right_t, left_c, right_c, own_c
    )

    near_t, near_c = [own_t, left_t, right_t], [own_c, left_c, right_c]
    pair_t, pair_c = [swap(p) for p in near_t], [swap(p) for p in near_c]
    pair_t, pair_c, near_t, near_c, far_t = fence(pair_t, pair_c, near_t, near_c, far_t)

    opp_t, opp_c = move(near_t[1], X_UP), move(near_c[2], X_DOWN)
    far_left_t, far_right_t = neighbours(far_t)
    far_c = move(near_c[0], FAR_Z)
    kept = forward(0, [near_t, pair_t], gate, up)
    weighted = weigh(0, [near_c, pair_c], me)
    opp_t, opp_c, far_left_t, far_right_t, far_c, far_t, weighted, kept = fence(
        opp_t, opp_c, far_left_t, far_right_t, far_c, far_t, weighted, kept
    )

    far_left_c, far_right_c = neighbours(far_c)
    far_near_t = [far_t, far_left_t, far_right_t]
    far_pair_t = [swap(p) for p in far_near_t]
    other = (1 - side).astype(jnp.int32)[None]
    kept, weighted, total = fence(kept, weighted, early_down(other, kept[1], weighted[0], 0, 2))
    kept = forward(2, [far_near_t], gate, up, kept)
    far_left_c, far_right_c, far_pair_t, far_left_t, far_c, kept, weighted, total = fence(
        far_left_c, far_right_c, far_pair_t, far_left_t, far_c, kept, weighted, total
    )

    far_opp_t, far_opp_c = move(far_left_t, X_UP), move(far_right_c, X_DOWN)
    far_near_c = [far_c, far_left_c, far_right_c]
    far_pair_c = [swap(p) for p in far_near_c]
    (weighted,) = weigh(2, [far_near_c], me, weighted)
    kept, total = fence(kept, early_down(other, kept[1], weighted, 2, 1, (total,)))
    kept = forward(3, [far_pair_t], gate, up, kept)
    far_opp_t, far_opp_c, far_pair_c, opp_t, opp_c, weighted, kept, total = fence(
        far_opp_t, far_opp_c, far_pair_c, opp_t, opp_c, weighted, kept, total
    )

    opp_pair_t, far_opp_pair_t = swap(opp_t), swap(far_opp_t)
    opp_pair_c, far_opp_pair_c = swap(opp_c), swap(far_opp_c)
    last_t = [[opp_t, opp_pair_t, far_opp_t, far_opp_pair_t]]
    all_tokens, hidden, a, b = forward(3, last_t, gate, up, kept)
    last_c = [far_pair_c, [opp_c, opp_pair_c], [far_opp_c, far_opp_pair_c]]
    weighted, sent_down = late_down(other, me, hidden, total, down, last_c, weighted)

    def half_of(matrix, which, axis=0):
        half = matrix.shape[axis] // 2
        return lax.dynamic_slice_in_dim(matrix, which * half, half, axis)

    def step(matrix, gradient):
        return (matrix.astype(jnp.float32) - LEARN_RATE * gradient).astype(jnp.bfloat16)

    def to_partner(block):
        return lax.ppermute(block, "rep", PARTNER)

    def new_down(which, weighted):
        grad = jnp.einsum(
            "rf,rd->fd", half_of(hidden, which, 1), weighted, preferred_element_type=jnp.float32
        )
        return step(half_of(down, which), grad * down_scale)

    def new_projection(matrix, which, grad_rows):
        grad = jnp.einsum(
            "rd,rf->df",
            half_of(all_tokens, which, 1),
            grad_rows,
            preferred_element_type=jnp.float32,
        )
        return step(half_of(matrix, which), grad * width_scale)

    got_down = to_partner(sent_down)
    gate_rows, up_rows = back(after(weighted, sent_down), down, a, b)
    sent_gate = new_projection(gate, 1 - side, gate_rows)
    got_gate = to_partner(sent_gate)
    up_rows, got_down, weighted, _ = lax.optimization_barrier(
        (up_rows, got_down, weighted, sent_gate)
    )
    sent_up = new_projection(up, 1 - side, up_rows)
    got_up = to_partner(sent_up)
    kept_down = after(new_down(side, after(weighted, sent_up)))
    mixed_down = average(kept_down, got_down)
    gate_rows, up_rows, got_gate, mixed_down = lax.optimization_barrier(
        (gate_rows, up_rows, got_gate, mixed_down)
    )
    kept_gate, kept_up = lax.optimization_barrier(
        (new_projection(gate, side, gate_rows), new_projection(up, side, up_rows))
    )
    mixed_gate = average(kept_gate, got_gate)
    mixed_up = average(kept_up, got_up)
    return (mixed_gate[None, None], mixed_up[None, None], mixed_down[None, None])


def solution(mesh):
    rows, matrices = P("rep", "exp", None), P("rep", "exp", None, None)
    return jax.shard_map(
        body,
        mesh=mesh,
        in_specs=(rows,) * 4 + (matrices,) * 3,
        out_specs=(matrices,) * 3,
        check_vma=False,
    )
```

```python
import functools

import jax
import jax.numpy as jnp
from jax import lax
from jax.experimental import pallas as pl
from jax.experimental.pallas import tpu as pltpu
from jax.sharding import PartitionSpec as P

ROUND = 2
LEARN_RATE = 2.0
EXPERTS = 16
TOK = 128
WIDTH = 2048
FF = 512
TABLE = 128
ROWS = 2048
EARLY = 1152


def exp_route(move):
    route = []
    for i in range(16):
        z, x, c = move(i // 8, (i // 2) % 4, i % 2)
        route.append((i, (z % 2) * 8 + (x % 4) * 2 + c % 2))
    return route


CORE = exp_route(lambda z, x, c: (z, x, c + 1))
FAR_Z = exp_route(lambda z, x, c: (z + 1, x, c))
X_UP = exp_route(lambda z, x, c: (z, x + 1, c))
X_DOWN = exp_route(lambda z, x, c: (z, x - 1, c))
PARTNER = [(r, r ^ (1 << ROUND)) for r in range(16)]


def move(block, route):
    return lax.ppermute(block, "exp", route)


def after(block, *deps):
    return lax.optimization_barrier((block,) + deps)[0]


def neighbours(block):
    return move(block, X_UP), move(block, X_DOWN)


def fence(*arrays):
    return lax.optimization_barrier(arrays)


def whole(shape):
    return pl.BlockSpec(shape, lambda *_: (0,) * len(shape), pipeline_mode=pl.Buffered(1))


HBM = pl.BlockSpec(memory_space=pl.ANY)
PARAMS = pltpu.CompilerParams(vmem_limit_bytes=64 * 2**20)


def chunk_call(kernel, base, groups, sides, side_specs, shapes, into, flops, n_held, splits):
    pieces = [piece for group in groups for piece in group]
    heights = [[piece.shape[0] for piece in group] for group in groups]
    chunk = sum(heights[0])
    n_in = len(pieces) + len(sides)
    blocked = [
        pl.BlockSpec((chunk, s.shape[1] // splits), lambda n, i: (base + i, n))
        for s in shapes[n_held:]
    ]
    return pl.pallas_call(
        functools.partial(kernel, base, heights, len(pieces), len(into)),
        grid=(splits, len(groups)),
        out_shape=shapes,
        in_specs=[HBM] * len(pieces) + side_specs + [HBM] * len(into),
        out_specs=[HBM] * n_held + blocked,
        scratch_shapes=[
            pltpu.VMEM((chunk * len(groups), pieces[0].shape[1]), jnp.bfloat16),
            pltpu.SemaphoreType.DMA((len(pieces),)),
            pltpu.SemaphoreType.DMA((len(groups),)),
        ],
        input_output_aliases={n_in + i: i for i in range(len(into))},
        compiler_params=PARAMS,
        cost_estimate=pl.CostEstimate(
            flops=flops * chunk * len(groups),
            bytes_accessed=4 * sum(p.size for p in pieces),
            transcendentals=0,
        ),
    )(*pieces, *sides, *into)


def fetch(heights, pieces, rows, sems, then=lambda g: None):
    copies, at = [], 0
    for group in heights:
        copies.append([])
        for n in group:
            i = len(sum(copies, []))
            copies[-1].append(
                pltpu.make_async_copy(pieces[i], rows.at[pl.ds(at, n), :], sems.at[i])
            )
            at += n
    first, step = pl.program_id(0) == 0, pl.program_id(1)

    @pl.when(first & (step == 0))
    def _():
        for group in copies:
            for copy in group:
                copy.start()

    for g, group in enumerate(copies):

        @pl.when(first & (step == g))
        def _():
            for copy in group:
                copy.wait()
            then(g)


def forward_kernel(base, heights, n_pieces, n_into, *refs):
    pieces, gate, up = refs[:n_pieces], refs[n_pieces], refs[n_pieces + 1]
    rows_out, hidden_ref, a_ref, b_ref, held, sems, out_sems = refs[n_pieces + 2 + n_into :]
    chunk = sum(heights[0])
    copies = [
        pltpu.make_async_copy(
            held.at[pl.ds(g * chunk, chunk), :],
            rows_out.at[pl.ds((base + g) * chunk, chunk), :],
            out_sems.at[g],
        )
        for g in range(len(heights))
    ]
    fetch(heights, pieces, held, sems, lambda g: copies[g].start())
    step = pl.program_id(1)
    rows = held[pl.ds(pl.multiple_of(step * chunk, chunk), chunk), :]
    gate_pre = jnp.dot(rows, gate[...], preferred_element_type=jnp.float32) * WIDTH**-0.5
    up_pre = jnp.dot(rows, up[...], preferred_element_type=jnp.float32) * WIDTH**-0.5
    sigmoid = jax.nn.sigmoid(gate_pre)
    silu = gate_pre * sigmoid
    hidden_ref[...] = (silu * up_pre).astype(jnp.bfloat16)
    a_ref[...] = up_pre * sigmoid * (1.0 + gate_pre * (1.0 - sigmoid))
    b_ref[...] = silu

    @pl.when((pl.program_id(0) == pl.num_programs(0) - 1) & (step == len(heights) - 1))
    def _():
        for copy in copies:
            copy.wait()


def forward(base, groups, gate, up, into=()):
    shapes = [
        jax.ShapeDtypeStruct((ROWS, WIDTH), jnp.bfloat16),
        jax.ShapeDtypeStruct((ROWS, FF), jnp.bfloat16),
        jax.ShapeDtypeStruct((ROWS, FF), jnp.float32),
        jax.ShapeDtypeStruct((ROWS, FF), jnp.float32),
    ]
    splits = 2 if len(groups) == 1 else 1
    specs = [pl.BlockSpec((WIDTH, FF // splits), lambda n, i: (0, n))] * 2
    return chunk_call(
        forward_kernel, base, groups, (gate, up), specs, shapes, into, 4 * WIDTH * FF, 1, splits
    )


def row_weight(table, me):
    lane = lax.broadcasted_iota(jnp.int32, table.shape, 1)
    mine = (lane % EXPERTS == me) & (lane < 3 * EXPERTS)
    return jnp.sum(jnp.where(mine, table.astype(jnp.float32), 0.0), axis=1, keepdims=True)


def weigh_kernel(base, heights, n_pieces, n_into, *refs):
    pieces, me_ref = refs[:n_pieces], refs[n_pieces]
    out, held, sems, _ = refs[n_pieces + 1 + n_into :]
    chunk = sum(heights[0])
    fetch(heights, pieces, held, sems)
    at = pl.ds(pl.multiple_of(pl.program_id(1) * chunk, chunk), chunk)
    weight = row_weight(held[at, WIDTH:], me_ref[0])
    out[...] = (held[at, :WIDTH].astype(jnp.float32) * weight).astype(jnp.bfloat16)


def weigh(base, groups, me, into=()):
    shapes = [jax.ShapeDtypeStruct((ROWS, WIDTH), jnp.bfloat16)]
    specs = [pl.BlockSpec(memory_space=pltpu.SMEM)]
    return chunk_call(
        weigh_kernel, base, groups, (me,), specs, shapes, into, 4 * WIDTH, 0, 1
    )


def label_kernel(cotangent_ref, routes_ref, weights_ref, own_ref):
    row = lax.broadcasted_iota(jnp.int32, (TABLE, TOK), 0)
    dense = jnp.zeros((TABLE, TOK), jnp.float32)
    for j in range(routes_ref.shape[0]):
        hit = routes_ref[j : j + 1, :] == row % EXPERTS
        dense += jnp.where(hit, weights_ref[j : j + 1, :], 0.0)
    high = dense.astype(jnp.bfloat16).astype(jnp.float32)
    middle = (dense - high).astype(jnp.bfloat16).astype(jnp.float32)
    low = (dense - high) - middle
    part = row // EXPERTS
    table = jnp.where(part == 0, high, jnp.where(part == 1, middle, low))
    own_ref[:, :WIDTH] = cotangent_ref[...]
    own_ref[:, WIDTH:] = jnp.where(part < 3, table, 0.0).T.astype(jnp.bfloat16)


def label(cotangent, routes, route_weights):
    return pl.pallas_call(
        label_kernel,
        out_shape=jax.ShapeDtypeStruct((TOK, WIDTH + TABLE), jnp.bfloat16),
        cost_estimate=pl.CostEstimate(flops=2**20, bytes_accessed=2**20, transcendentals=0),
    )(cotangent, routes.T, route_weights.T)


def transposed_dot(left, right):
    return lax.dot_general(
        left, right, (((0,), (0,)), ((), ())), preferred_element_type=jnp.float32
    )


def early_down_kernel(which_ref, hidden_ref, weighted_ref, *refs):
    before, total_ref = refs[:-1], refs[-1]

    @pl.when(pl.program_id(0) == 0)
    def _():
        total_ref[...] = before[0][...] if before else jnp.zeros_like(total_ref)

    total_ref[...] += transposed_dot(hidden_ref[...], weighted_ref[...])


def early_down(which, hidden, weighted, first, count, before=()):
    chunk, half = EARLY // 3, FF // 2
    result = pl.BlockSpec((half, WIDTH), lambda i, which: (0, 0))
    return pl.pallas_call(
        early_down_kernel,
        grid_spec=pltpu.PrefetchScalarGridSpec(
            num_scalar_prefetch=1,
            grid=(count,),
            in_specs=[
                pl.BlockSpec((chunk, half), lambda i, which: (first + i, which[0])),
                pl.BlockSpec((chunk, WIDTH), lambda i, which: (first + i, 0)),
            ]
            + [result] * len(before),
            out_specs=result,
        ),
        out_shape=jax.ShapeDtypeStruct((half, WIDTH), jnp.float32),
        compiler_params=PARAMS,
        cost_estimate=pl.CostEstimate(flops=2**22, bytes_accessed=2**22, transcendentals=0),
    )(which, hidden, weighted, *before)


def late_down_kernel(groups, which_ref, me_ref, hidden_ref, total_ref, down_ref, *refs):
    n = sum(groups)
    pieces, rest = refs[:n], refs[n:]
    _, out_ref, sent_ref, held, rows, hidden, before, matrix, sems, out_sems, side_sems = rest
    half = FF // 2
    at = pl.ds(pl.multiple_of(which_ref[0] * half, half), half)
    sides = [
        pltpu.make_async_copy(hidden_ref.at[pl.ds(EARLY, ROWS - EARLY), at], hidden, side_sems.at[0]),
        pltpu.make_async_copy(total_ref, before, side_sems.at[1]),
        pltpu.make_async_copy(down_ref.at[at, :], matrix, side_sems.at[2]),
    ]
    copies = [
        pltpu.make_async_copy(piece, held.at[pl.ds(i * TOK, TOK), :], sems.at[i])
        for i, piece in enumerate(pieces)
    ]
    for copy in copies + sides:
        copy.start()
    total, first, leaves = None, 0, []
    for g, count in enumerate(groups):
        for copy in copies[first : first + count]:
            copy.wait()
        at = pl.ds(first * TOK, count * TOK)
        weight = row_weight(held[at, WIDTH:], me_ref[0])
        rows[at, :] = (held[at, :WIDTH].astype(jnp.float32) * weight).astype(jnp.bfloat16)
        leaves.append(
            pltpu.make_async_copy(
                rows.at[at, :],
                out_ref.at[pl.ds(EARLY + first * TOK, count * TOK), :],
                out_sems.at[g],
            )
        )
        leaves[-1].start()
        if total is None:
            sides[0].wait()
            sides[1].wait()
            total = before[...]
        total += transposed_dot(hidden[at, :], rows[at, :])
        first += count
    sides[2].wait()
    old = matrix[...].astype(jnp.float32)
    sent_ref[...] = (old - LEARN_RATE * (total * FF**-0.5)).astype(jnp.bfloat16)
    for leave in leaves:
        leave.wait()


def late_down(which, me, hidden, total, down, groups, weighted):
    pieces = [piece for group in groups for piece in group]
    half, count = FF // 2, ROWS - EARLY
    return pl.pallas_call(
        functools.partial(late_down_kernel, [len(group) for group in groups]),
        grid_spec=pltpu.PrefetchScalarGridSpec(
            num_scalar_prefetch=1,
            grid=(1,),
            in_specs=[
                pl.BlockSpec(memory_space=pltpu.SMEM),
            ]
            + [HBM] * (len(pieces) + 4),
            out_specs=[HBM, pl.BlockSpec((half, WIDTH), lambda i, which: (0, 0))],
            scratch_shapes=[
                pltpu.VMEM((count, WIDTH + TABLE), jnp.bfloat16),
                pltpu.VMEM((count, WIDTH), jnp.bfloat16),
                pltpu.VMEM((count, half), jnp.bfloat16),
                pltpu.VMEM((half, WIDTH), jnp.float32),
                pltpu.VMEM((half, WIDTH), jnp.bfloat16),
                pltpu.SemaphoreType.DMA((len(pieces),)),
                pltpu.SemaphoreType.DMA((len(groups),)),
                pltpu.SemaphoreType.DMA((3,)),
            ],
        ),
        out_shape=[
            jax.ShapeDtypeStruct((ROWS, WIDTH), jnp.bfloat16),
            jax.ShapeDtypeStruct((half, WIDTH), jnp.bfloat16),
        ],
        input_output_aliases={5 + len(pieces): 0},
        compiler_params=PARAMS,
        cost_estimate=pl.CostEstimate(flops=2**22, bytes_accessed=2**22, transcendentals=0),
    )(which, me, hidden, total, down, *pieces, weighted)


def back_kernel(weighted_ref, down_ref, a_ref, b_ref, gate_ref, up_ref):
    hidden_grad = FF**-0.5 * lax.dot_general(
        weighted_ref[...],
        down_ref[...],
        (((1,), (1,)), ((), ())),
        preferred_element_type=jnp.float32,
    )
    gate_ref[...] = (hidden_grad * a_ref[...]).astype(jnp.bfloat16)
    up_ref[...] = (hidden_grad * b_ref[...]).astype(jnp.bfloat16)


def back(weighted, down, a, b):
    chunk = 512
    rows = pl.BlockSpec((chunk, WIDTH), lambda i: (i, 0))
    narrow = pl.BlockSpec((chunk, FF), lambda i: (i, 0))
    return pl.pallas_call(
        back_kernel,
        grid=(ROWS // chunk,),
        out_shape=[jax.ShapeDtypeStruct((ROWS, FF), jnp.bfloat16)] * 2,
        in_specs=[rows, whole(down.shape), narrow, narrow],
        out_specs=[narrow, narrow],
        compiler_params=PARAMS,
        cost_estimate=pl.CostEstimate(flops=2**20, bytes_accessed=2**20, transcendentals=0),
    )(weighted, down, a, b)


def average(kept, received):
    return (0.5 * (kept.astype(jnp.float32) + received.astype(jnp.float32))).astype(jnp.bfloat16)


def body(tokens, cotangent, routes, route_weights, gate_weight, up_weight, down_weight):
    own_t, own_c = tokens[0], cotangent[0]
    gate, up, down = gate_weight[0, 0], up_weight[0, 0], down_weight[0, 0]
    width_scale, down_scale = WIDTH**-0.5, FF**-0.5
    me = lax.axis_index("exp").astype(jnp.int32)[None]
    side = jnp.bitwise_and(jnp.right_shift(lax.axis_index("rep"), ROUND), 1)

    own_c = label(own_c, routes[0], route_weights[0])

    def swap(block):
        return move(block, CORE)

    far_t = move(after(own_t, own_c), FAR_Z)
    left_t, right_t = neighbours(own_t)
    left_c, right_c = neighbours(own_c)
    far_t, left_t, right_t, left_c, right_c, own_c = fence(
        far_t, left_t, right_t, left_c, right_c, own_c
    )

    near_t, near_c = [own_t, left_t, right_t], [own_c, left_c, right_c]
    pair_t, pair_c = [swap(p) for p in near_t], [swap(p) for p in near_c]
    pair_t, pair_c, near_t, near_c, far_t = fence(pair_t, pair_c, near_t, near_c, far_t)

    opp_t, opp_c = move(near_t[1], X_UP), move(near_c[2], X_DOWN)
    far_left_t, far_right_t = neighbours(far_t)
    far_c = move(own_c, FAR_Z)
    kept = forward(0, [near_t, pair_t], gate, up)
    weighted = weigh(0, [near_c, pair_c], me)
    opp_t, opp_c, far_left_t, far_right_t, far_c, far_t, weighted, kept = fence(
        opp_t, opp_c, far_left_t, far_right_t, far_c, far_t, weighted, kept
    )

    far_left_c, far_right_c = neighbours(far_c)
    far_near_t = [far_t, far_left_t, far_right_t]
    far_pair_t = [swap(p) for p in far_near_t]
    other = (1 - side).astype(jnp.int32)[None]
    kept, weighted, total = fence(kept, weighted, early_down(other, kept[1], weighted[0], 0, 2))
    kept = forward(2, [far_near_t], gate, up, kept)
    far_left_c, far_right_c, far_pair_t, far_left_t, far_c, kept, weighted, total = fence(
        far_left_c, far_right_c, far_pair_t, far_left_t, far_c, kept, weighted, total
    )

    far_opp_t, far_opp_c = move(far_left_t, X_UP), move(far_right_c, X_DOWN)
    far_near_c = [far_c, far_left_c, far_right_c]
    far_pair_c = [swap(p) for p in far_near_c]
    (weighted,) = weigh(2, [far_near_c], me, weighted)
    kept, total = fence(kept, early_down(other, kept[1], weighted, 2, 1, (total,)))
    kept = forward(3, [far_pair_t], gate, up, kept)
    far_opp_t, far_opp_c, far_pair_c, opp_t, opp_c, weighted, kept, total = fence(
        far_opp_t, far_opp_c, far_pair_c, opp_t, opp_c, weighted, kept, total
    )

    opp_pair_t, far_opp_pair_t = swap(opp_t), swap(far_opp_t)
    opp_pair_c, far_opp_pair_c = swap(opp_c), swap(far_opp_c)
    last_t = [[opp_t, opp_pair_t, far_opp_t, far_opp_pair_t]]
    all_tokens, hidden, a, b = forward(3, last_t, gate, up, kept)
    last_c = [far_pair_c, [opp_c, opp_pair_c], [far_opp_c, far_opp_pair_c]]
    weighted, sent_down = late_down(other, me, hidden, total, down, last_c, weighted)

    def half_of(matrix, which, axis=0):
        half = matrix.shape[axis] // 2
        return lax.dynamic_slice_in_dim(matrix, which * half, half, axis)

    def step(matrix, gradient):
        return (matrix.astype(jnp.float32) - LEARN_RATE * gradient).astype(jnp.bfloat16)

    def to_partner(block):
        return lax.ppermute(block, "rep", PARTNER)

    def new_down(which, weighted):
        grad = jnp.einsum(
            "rf,rd->fd", half_of(hidden, which, 1), weighted, preferred_element_type=jnp.float32
        )
        return step(half_of(down, which), grad * down_scale)

    def new_projection(matrix, which, grad_rows):
        grad = jnp.einsum(
            "rd,rf->df",
            half_of(all_tokens, which, 1),
            grad_rows,
            preferred_element_type=jnp.float32,
        )
        return step(half_of(matrix, which), grad * width_scale)

    got_down = to_partner(sent_down)
    gate_rows, up_rows = back(after(weighted, sent_down), down, a, b)
    sent_gate = new_projection(gate, 1 - side, gate_rows)
    got_gate = to_partner(sent_gate)
    up_rows, got_down, weighted, _ = lax.optimization_barrier(
        (up_rows, got_down, weighted, sent_gate)
    )
    sent_up = new_projection(up, 1 - side, up_rows)
    got_up = to_partner(sent_up)
    kept_down = after(new_down(side, after(weighted, sent_up)))
    mixed_down = average(kept_down, got_down)
    gate_rows, up_rows, got_gate, mixed_down = lax.optimization_barrier(
        (gate_rows, up_rows, got_gate, mixed_down)
    )
    kept_gate, kept_up = lax.optimization_barrier(
        (new_projection(gate, side, gate_rows), new_projection(up, side, up_rows))
    )
    mixed_gate = average(kept_gate, got_gate)
    mixed_up = average(kept_up, got_up)
    return (mixed_gate[None, None], mixed_up[None, None], mixed_down[None, None])


def solution(mesh):
    rows, matrices = P("rep", "exp", None), P("rep", "exp", None, None)
    return jax.shard_map(
        body,
        mesh=mesh,
        in_specs=(rows,) * 4 + (matrices,) * 3,
        out_specs=(matrices,) * 3,
        check_vma=False,
    )
```
